128 devices in a mesh: grp: 2 (over core), row: 4 (over z), col: 16 (over y, x).
Axes of the slice: x: 4, y: 4, z: 4, core: 2. Of those that a mesh axis runs over, the one named last changes fastest.
Arguments:
- jacobian: float32 [512, 16384], P(('grp', 'row', 'col')), may hold values from -0.25 to 0.25
- covariance: float32 [16384, 8192], P(('grp', 'row'), 'col'), as said below
- noise: float32 [512], replicated, may hold values from 0.5 to 2
- innovation: float32 [512], replicated, may hold values from -36 to 36
Outputs:
- delta: float32 [16384], P(('grp', 'row'))
- new_covariance: float32 [16384, 8192], P(('grp', 'row'), 'col')
The draws below stay inside these ranges and needn't reach their ends.
Inputs may be any that keep to these rules, and one draw needn't show every extreme that they name: Each block of 8192 rows of covariance is symmetric and positive definite.
All inputs are finite; a program needn't handle non-finite values.
Results may differ from the reference program's by a relative error of at most 0.00075.
Values sent between devices are 32-bit elements; how exact they have to be, the bound alone decides.
No kernel may reach another device: no remote copies, remote signals or barrier semaphores. Data moves between devices by JAX's collectives and lax.ppermute only.
A program may use at most 64 MiB of HBM per device.

```python
import math
import jax
import jax.numpy as jnp
from jax import lax

NB = 8192
M = 512
GROUPS = 2
NP = 16384


def draw_jacobian(key, part):
    key = jax.random.fold_in(key, 23)
    first, second = jax.random.split(key, 2)
    base = jnp.clip(jax.random.normal(first, (M, NP), jnp.float32), -6.0, 6.0)
    low_scale = 0.1
    high_scale = 15.0
    base = base * (1.0 / NB ** 0.5)
    order = jax.random.permutation(second, M).astype(jnp.float32)
    fraction = order / (M - 1.0)
    row_scales = jnp.exp(jnp.log(low_scale) + fraction * (jnp.log(high_scale) - jnp.log(low_scale)))
    mixed = base * row_scales[:, None]
    width = 1
    while width < M:
        paired = mixed.reshape(M // (2 * width), 2, width, NP)
        upper = paired[:, 0]
        lower = paired[:, 1]
        mixed = jnp.stack([upper + lower, upper - lower], axis=1).reshape(M, NP)
        width = width * 2
    mixed = mixed * (1.0 / M ** 0.5)
    return jnp.clip(mixed, -0.25, 0.25).astype(jnp.float32)


def draw_covariance(key, part):
    first, second, third = jax.random.split(jax.random.fold_in(key, 11), 3)
    low_diag = 1.0
    high_diag = 2.0
    spread = 0.75
    low_scale = 0.7
    high_scale = 1.5
    amplitude = spread / NB ** 0.5
    raw = jax.random.uniform(first, (GROUPS, NB, NB), jnp.float32, -1.0, 1.0)
    raw = 0.5 * (raw + jnp.swapaxes(raw, 1, 2)) * amplitude
    diagonal = jnp.exp(jax.random.uniform(second, (GROUPS, NB, 1), jnp.float32, jnp.log(low_diag), jnp.log(high_diag)))
    scales = jnp.exp(jax.random.uniform(third, (GROUPS, NB, 1), jnp.float32, jnp.log(low_scale), jnp.log(high_scale)))
    rows_index = lax.broadcasted_iota(jnp.int32, (1, NB, NB), 1)
    cols_index = lax.broadcasted_iota(jnp.int32, (1, NB, NB), 2)
    reach = NB / 8.0
    distance = jnp.abs(rows_index - cols_index).astype(jnp.float32)
    kernel = scales * jnp.swapaxes(scales, 1, 2) * jnp.exp(-distance / reach)
    full = jnp.where(rows_index == cols_index, diagonal + kernel, raw + kernel)
    return full.reshape(GROUPS * NB, NB).astype(jnp.float32)


def scatter_about(stream_key, dims, deviation, limit, dtype=jnp.bfloat16):
    result = jax.random.normal(stream_key, dims, jnp.float32) * deviation
    return jnp.minimum(jnp.maximum(result, -limit), limit).astype(dtype)


def setup_inputs(seed: int = 0) -> dict:
    seeds = jax.random.split(jax.random.key(seed), 5)
    jacobian = draw_jacobian(jax.random.fold_in(seeds[4], 71), 0)
    covariance = draw_covariance(jax.random.fold_in(seeds[4], 71), 0)
    noise = jnp.clip(jnp.exp(jax.random.uniform(seeds[2], (M,), jnp.float32, math.log(0.5), math.log(2.0))), 0.5, 2.0)
    innovation = scatter_about(seeds[3], (M,), 6.0, 36.0, jnp.float32)
    return dict(jacobian=jacobian, covariance=covariance, noise=noise, innovation=innovation)


def reference(jacobian, covariance, noise, innovation):
    high = lax.Precision.HIGHEST
    products = []
    blocks = []
    system = jnp.diag(noise).astype(jnp.float32)
    for group in range(GROUPS):
        jac_block = jacobian[:, group * NB:(group + 1) * NB]
        cov_block = covariance[group * NB:(group + 1) * NB]
        product = jnp.dot(jac_block.astype(jnp.float32), cov_block.astype(jnp.float32), precision=high, preferred_element_type=jnp.float32)
        products.append(product)
        blocks.append(cov_block)
        system = system + jnp.dot(product.astype(jnp.float32), jac_block.T.astype(jnp.float32), precision=high, preferred_element_type=jnp.float32)
    lower = jnp.linalg.cholesky(system)
    solve_e = jax.scipy.linalg.cho_solve((lower, True), innovation)
    deltas = []
    updated = []
    for group in range(GROUPS):
        product = products[group]
        solved = jax.scipy.linalg.cho_solve((lower, True), product)
        change = jnp.dot(product.T.astype(jnp.float32), solved.astype(jnp.float32), precision=high, preferred_element_type=jnp.float32)
        updated.append((blocks[group] - change) / 0.98)
        deltas.append(jnp.dot(product.T.astype(jnp.float32), solve_e.astype(jnp.float32), precision=high, preferred_element_type=jnp.float32))
    return (jnp.concatenate(deltas), jnp.concatenate(updated, axis=0))
```

```python
import jax
import jax.numpy as jnp
from jax import lax
from jax.experimental import pallas as pl
from jax.experimental.pallas import tpu as pltpu
from jax.sharding import PartitionSpec as P

HI = lax.Precision.HIGHEST
B = 128
Q = 8
Z = 4
YX = 4


def dot6(a, b):
    return jnp.dot(a, b, precision=HI, preferred_element_type=jnp.float32)


def sweep_block(a):
    n = B // Q
    rows = [a[Q * i:Q * i + Q, :] for i in range(n)]
    lane = lax.broadcasted_iota(jnp.int32, (Q, B), 1)
    sub = lax.broadcasted_iota(jnp.int32, (Q, B), 0)
    for p in range(n):
        r = rows[p]
        cols = [jnp.broadcast_to(r[:, Q * p + j:Q * p + j + 1], (Q, B)) for j in range(Q)]
        for k in range(Q):
            inv = 1.0 / jnp.broadcast_to(cols[k][k:k + 1, :], (Q, B))
            scaled = cols[k] * inv
            new = []
            for j in range(Q):
                if j == k:
                    new.append(jnp.where(sub == k, -inv, scaled))
                else:
                    row = jnp.broadcast_to(cols[j][k:k + 1, :], (Q, B))
                    new.append(jnp.where(sub == k, row * inv, cols[j] - scaled * row))
            row = jnp.broadcast_to(r[k:k + 1, :], (Q, B))
            r = jnp.where(sub == k, row * inv, r - scaled * row)
            cols = new
        for j in range(Q):
            r = jnp.where(lane == Q * p + j, cols[j], r)
        inside = (lane >= Q * p) & (lane < Q * p + Q)
        splat = [jnp.broadcast_to(r[j:j + 1, :], (Q, B)) for j in range(Q)]
        for b in [(p + 1 + i) % n for i in range(n - 1)]:
            old = rows[b]
            acc = jnp.where(inside, 0.0, old)
            for j in range(Q):
                acc = acc - jnp.broadcast_to(old[:, Q * p + j:Q * p + j + 1], (Q, B)) * splat[j]
            rows[b] = acc
        rows[p] = r
    return jnp.concatenate(rows, axis=0)


def inverse_kernel(s_ref, noise_ref, out_ref):
    m = out_ref.shape[0]
    n = m // B
    row_id = lax.broadcasted_iota(jnp.int32, (m, m), 0)
    col_id = lax.broadcasted_iota(jnp.int32, (m, m), 1)
    out_ref[...] = s_ref[...] + jnp.where(row_id == col_id, noise_ref[...], 0.0)

    def step(k, carry):
        at = pl.ds(pl.multiple_of(k * B, B), B)
        neg = sweep_block(out_ref[at, at])
        strip = out_ref[at, :]
        left = out_ref[:, at]
        col = lax.broadcasted_iota(jnp.int32, (B, m), 1)
        here = (col >= k * B) & (col < k * B + B)
        t = jnp.where(here, jnp.concatenate([neg] * n, axis=1), -dot6(neg, strip))
        big = lax.broadcasted_iota(jnp.int32, (m, m), 1)
        keep = jnp.where((big >= k * B) & (big < k * B + B), 0.0, out_ref[...])
        out_ref[...] = keep - dot6(left, t)
        out_ref[at, :] = t
        return carry

    lax.fori_loop(0, n, step, 0)


def negative_inverse(system, noise):
    vmem = pl.BlockSpec(memory_space=pltpu.VMEM)
    return pl.pallas_call(
        inverse_kernel,
        out_shape=jax.ShapeDtypeStruct(system.shape, jnp.float32),
        in_specs=[vmem, vmem],
        out_specs=vmem,
        compiler_params=pltpu.CompilerParams(vmem_limit_bytes=24 * 2**20),
        name="inverse",
    )(system, noise)


def split(a):
    high = a.astype(jnp.bfloat16)
    return high, (a - high.astype(jnp.float32)).astype(jnp.bfloat16)


def final_kernel(z_ref, neg_ref, innov_ref, p0, p1, p2, p3, rows_ref, cov_ref, new_ref, delta_ref, yh, yl, u):
    @pl.when(pl.program_id(0) == 0)
    def _():
        neg = neg_ref[...]
        for j, piece in enumerate((p0, p1, p2, p3)):
            place = lax.rem(z_ref[0] + (Z - j), Z)
            at = pl.ds(pl.multiple_of(place * B, B), B)
            yh[:, at], yl[:, at] = split(dot6(neg, piece[...]))
        u[...] = -jnp.sum(neg * innov_ref[...], axis=1, keepdims=True)

    chunk = rows_ref[0]
    ch, cl = split(chunk)

    def tdot(a, b):
        return lax.dot_general(a, b, (((0,), (0,)), ((), ())), preferred_element_type=jnp.float32)

    change = tdot(ch, yh[...]) + (tdot(ch, yl[...]) + tdot(cl, yh[...]))
    new_ref[...] = (cov_ref[...] + change) / 0.98
    delta_ref[0] = jnp.sum(chunk * u[...], axis=0, keepdims=True)


def finish(z, neg, innovation, pieces, prod_rows, covariance):
    m = neg.shape[0]
    rows_dev, cols_dev = covariance.shape
    whole = lambda *shape: pl.BlockSpec(shape, lambda i: (0,) * len(shape))
    place = lambda i: (i % YX) * Z + i // YX
    new, delta = pl.pallas_call(
        final_kernel,
        grid=(rows_dev // B,),
        out_shape=(
            jax.ShapeDtypeStruct((rows_dev, cols_dev), jnp.float32),
            jax.ShapeDtypeStruct((rows_dev // B, 1, B), jnp.float32),
        ),
        in_specs=[
            pl.BlockSpec(memory_space=pltpu.SMEM),
            whole(m, m),
            whole(1, m),
            *[whole(m, B)] * 4,
            pl.BlockSpec((1, m, B), lambda i: (i, 0, 0)),
            pl.BlockSpec((B, cols_dev), lambda i: (place(i), 0)),
        ],
        out_specs=(
            pl.BlockSpec((B, cols_dev), lambda i: (place(i), 0)),
            pl.BlockSpec((1, 1, B), lambda i: (place(i), 0, 0)),
        ),
        scratch_shapes=[
            pltpu.VMEM((m, cols_dev), jnp.bfloat16),
            pltpu.VMEM((m, cols_dev), jnp.bfloat16),
            pltpu.VMEM((m, 1), jnp.float32),
        ],
        compiler_params=pltpu.CompilerParams(vmem_limit_bytes=24 * 2**20),
        name="finish",
    )(z, neg, innovation, *pieces, prod_rows, covariance)
    return delta.reshape(rows_dev), new


def exchange(value, axes):
    return lax.all_to_all(value, axes, split_axis=0, concat_axis=0, tiled=True)


def per_device(jacobian, covariance, noise, innovation):
    m = noise.shape[0]
    mine = jacobian.shape[0]
    rows_dev, cols_dev = covariance.shape
    g = lax.axis_index("grp")
    z = lax.axis_index("row")
    reorder = lambda v: v.reshape(8, 16, mine).transpose(1, 0, 2).reshape(1, m)
    noise, innovation = reorder(noise), reorder(innovation)

    sent = jacobian.reshape(mine, 8, rows_dev).transpose(1, 0, 2)
    part = exchange(sent, ("grp", "row")).reshape(8 * mine, rows_dev)
    jac_rows = lax.all_gather(part, "col", axis=0, tiled=True)

    sent = jacobian.reshape(mine, 2, 16, Z, B).transpose(1, 3, 2, 0, 4).reshape(128, mine, B)
    piece = exchange(sent, ("grp", "row", "col")).reshape(8, 16, mine, B)
    piece = piece.transpose(1, 0, 2, 3).reshape(1, m, B)
    jac_cols = exchange(jnp.broadcast_to(piece, (Z, m, B)), ("row",))
    jac_cols = jac_cols.transpose(1, 0, 2).reshape(m, cols_dev)

    partial = jnp.dot(jac_rows, covariance, precision=HI, preferred_element_type=jnp.float32)
    system = jnp.dot(partial, jac_cols.T, precision=HI, preferred_element_type=jnp.float32)

    half = m // 2
    swap = [(0, 1), (1, 0)]
    own = lax.dynamic_slice_in_dim(system, g * half, half, 0)
    other = lax.dynamic_slice_in_dim(system, (1 - g) * half, half, 0)
    own = own + lax.ppermute(other, "grp", swap)
    got = exchange(own.reshape(64, half // 64, m), ("row", "col"))
    share = jnp.sum(got, axis=0, keepdims=True)
    own = exchange(jnp.broadcast_to(share, (64, half // 64, m)), ("row", "col")).reshape(half, m)
    other = lax.ppermute(own, "grp", swap)
    first = jnp.where(g == 0, own, other)
    second = jnp.where(g == 0, other, own)
    neg = negative_inverse(jnp.concatenate([first, second], axis=0), noise)

    spots = [(a, b, x) for a in range(Z) for b in range(YX) for x in range(YX)]
    number = lambda a, b, x: (a * YX + b) * YX + x
    total = None
    for j in range(Z):
        sub = lax.rem(z + j, Z)
        out = lax.dynamic_slice_in_dim(partial, sub * B, B, 1)
        perm = [(number(a, b, x), number(b, (a + j) % Z, x)) for a, b, x in spots]
        came = lax.ppermute(out, ("row", "col"), perm)
        total = came if total is None else total + came
    prod_rows = lax.all_gather(total, "col", axis=0)
    pieces = []
    for j in range(Z):
        perm = [(number(a, b, x), number((b + j) % Z, a, x)) for a, b, x in spots]
        pieces.append(lax.ppermute(total, ("row", "col"), perm))

    return finish(z.reshape(1), neg, innovation, pieces, prod_rows, covariance)


def solution(mesh):
    in_specs = (P(("grp", "row", "col"), None), P(("grp", "row"), "col"), P(), P())
    out_specs = (P(("grp", "row")), P(("grp", "row"), "col"))
    return jax.shard_map(
        per_device, mesh=mesh, in_specs=in_specs, out_specs=out_specs, check_vma=False
    )
```

```python
import functools

import jax
import jax.numpy as jnp
from jax import lax
from jax.experimental import pallas as pl
from jax.experimental.pallas import tpu as pltpu
from jax.sharding import PartitionSpec as P

HI = lax.Precision.HIGHEST
B = 128
Q = 8
RING = 4
SHIFT = (0, -1, 1, 2)


def dot6(a, b):
    return jnp.dot(a, b, precision=HI, preferred_element_type=jnp.float32)


def sweep_block(a):
    n = B // Q
    rows = [a[Q * i:Q * i + Q, :] for i in range(n)]
    lane = lax.broadcasted_iota(jnp.int32, (Q, B), 1)
    sub = lax.broadcasted_iota(jnp.int32, (Q, B), 0)
    for p in range(n):
        r = rows[p]
        cols = [jnp.broadcast_to(r[:, Q * p + j:Q * p + j + 1], (Q, B)) for j in range(Q)]
        for k in range(Q):
            inv = 1.0 / jnp.broadcast_to(cols[k][k:k + 1, :], (Q, B))
            scaled = cols[k] * inv
            new = []
            for j in range(Q):
                if j == k:
                    new.append(jnp.where(sub == k, -inv, scaled))
                else:
                    row = jnp.broadcast_to(cols[j][k:k + 1, :], (Q, B))
                    new.append(jnp.where(sub == k, row * inv, cols[j] - scaled * row))
            row = jnp.broadcast_to(r[k:k + 1, :], (Q, B))
            r = jnp.where(sub == k, row * inv, r - scaled * row)
            cols = new
        for j in range(Q):
            r = jnp.where(lane == Q * p + j, cols[j], r)
        inside = (lane >= Q * p) & (lane < Q * p + Q)
        splat = [jnp.broadcast_to(r[j:j + 1, :], (Q, B)) for j in range(Q)]
        for b in [(p + 1 + i) % n for i in range(n - 1)]:
            old = rows[b]
            acc = jnp.where(inside, 0.0, old)
            for j in range(Q):
                acc = acc - jnp.broadcast_to(old[:, Q * p + j:Q * p + j + 1], (Q, B)) * splat[j]
            rows[b] = acc
        rows[p] = r
    return jnp.concatenate(rows, axis=0)


def inverse_kernel(at_ref, own_ref, other_ref, noise_ref, out_ref):
    m = out_ref.shape[0]
    half = m // 2
    n = m // B
    g = at_ref[0]
    for source, start in ((own_ref, g * half), (other_ref, (1 - g) * half)):
        row_id = lax.broadcasted_iota(jnp.int32, (half, m), 0) + start
        col_id = lax.broadcasted_iota(jnp.int32, (half, m), 1)
        value = source[...] + jnp.where(row_id == col_id, noise_ref[...], 0.0)
        out_ref[pl.ds(pl.multiple_of(start, half), half), :] = value

    def step(k, carry):
        at = pl.ds(pl.multiple_of(k * B, B), B)
        neg = sweep_block(out_ref[at, at])
        strip = out_ref[at, :]
        left = out_ref[:, at]
        col = lax.broadcasted_iota(jnp.int32, (B, m), 1)
        here = (col >= k * B) & (col < k * B + B)
        t = jnp.where(here, jnp.concatenate([neg] * n, axis=1), -dot6(neg, strip))
        big = lax.broadcasted_iota(jnp.int32, (m, m), 1)
        keep = jnp.where((big >= k * B) & (big < k * B + B), 0.0, out_ref[...])
        out_ref[...] = keep - dot6(left, t)
        out_ref[at, :] = t
        return carry

    lax.fori_loop(0, n, step, 0)


VMEM = pl.BlockSpec(memory_space=pltpu.VMEM)
SMEM = pl.BlockSpec(memory_space=pltpu.SMEM)
PARAMS = pltpu.CompilerParams(vmem_limit_bytes=40 * 2**20)


def negative_inverse(at, own, other, noise):
    m = noise.shape[1]
    return pl.pallas_call(
        inverse_kernel,
        out_shape=jax.ShapeDtypeStruct((m, m), jnp.float32),
        in_specs=[SMEM, VMEM, VMEM, VMEM],
        out_specs=VMEM,
        compiler_params=PARAMS,
        cost_estimate=pl.CostEstimate(flops=20 * 10**9, bytes_accessed=2 * 2**20, transcendentals=0),
        name="inverse",
    )(at, own, other, noise)


def split(a):
    high = a.astype(jnp.bfloat16)
    return high, (a - high.astype(jnp.float32)).astype(jnp.bfloat16)


def split3(a):
    high = a.astype(jnp.bfloat16)
    rest = a - high.astype(jnp.float32)
    return (high, *split(rest))


def mul(a, b):
    return jnp.dot(a, b, preferred_element_type=jnp.float32)


def split_kernel(a_ref, *outs):
    for out, value in zip(outs, split3(a_ref[...])):
        out[...] = value


def split_array(a):
    rows, cols = a.shape
    spec = pl.BlockSpec((rows // 4, cols), lambda i: (i, 0))
    return pl.pallas_call(
        split_kernel,
        grid=(4,),
        out_shape=(jax.ShapeDtypeStruct(a.shape, jnp.bfloat16),) * 3,
        in_specs=[spec],
        out_specs=(spec,) * 3,
        compiler_params=PARAMS,
        name="split",
    )(a)


def product(chunks, parts):
    left = jnp.concatenate([c[...] for c in chunks], axis=0)
    ph, pm, pl_ = parts
    step = 512
    total = None
    for k in range(0, left.shape[1], step):
        jh, jm, jl = split3(left[:, k:k + step])
        h, mid, low = ph[k:k + step, :], pm[k:k + step, :], pl_[k:k + step, :]
        term = mul(jh, h) + ((mul(jh, mid) + mul(jm, h)) + (mul(jh, low) + mul(jm, mid) + mul(jl, h)))
        total = term if total is None else total + term
    return total


def product_kernel(n, *refs):
    refs[n + 3][...] = product(refs[:n], refs[n:n + 3])


def multiply(chunks, parts):
    rows = sum(c.shape[0] for c in chunks)
    cols = parts[0].shape[1]
    work = 12 * rows * cols * parts[0].shape[0]
    return pl.pallas_call(
        functools.partial(product_kernel, len(chunks)),
        out_shape=jax.ShapeDtypeStruct((rows, cols), jnp.float32),
        in_specs=[VMEM] * (len(chunks) + 3),
        out_specs=VMEM,
        compiler_params=PARAMS,
        cost_estimate=pl.CostEstimate(flops=work, bytes_accessed=8 * 2**20, transcendentals=0),
        name="multiply",
    )(*chunks, *parts)


def runs(y, x, own):
    def start(half, dy, dx):
        spot = lax.rem(y + (dy + RING), RING) * RING + lax.rem(x + (dx + RING), RING)
        return (half * RING * RING + spot) * own

    first = lambda step: [start(0, SHIFT[step], d) for d in SHIFT]
    second = lambda step: [start(1, d, SHIFT[step]) for d in SHIFT]
    early = first(0) + second(0)
    middle = first(1) + first(2) + second(1) + second(2)
    late = first(3) + second(3)
    return early, middle, late


def last_kernel(at_ref, c0, c1, c2, c3, ph, pm, pl_, early_ref, middle_ref, out_ref, late_ref):
    late_ref[...] = product((c0, c1, c2, c3), (ph, pm, pl_))
    own = out_ref.shape[1] // (2 * RING * RING)
    z = at_ref[1]
    for ref, starts in zip((early_ref, middle_ref, late_ref), runs(at_ref[2], at_ref[3], own)):
        for i, start in enumerate(starts):
            rows = pl.ds(pl.multiple_of(start, own), own)
            for j in range(RING):
                lanes = pl.ds(pl.multiple_of(lax.rem(z + j, RING) * B, B), B)
                out_ref[j, rows, :] = ref[i * own:(i + 1) * own, lanes]


def multiply_last(at, chunks, parts, early, middle):
    rows = sum(c.shape[0] for c in chunks)
    cols = parts[0].shape[1]
    m = rows + early.shape[0] + middle.shape[0]
    return pl.pallas_call(
        last_kernel,
        out_shape=jax.ShapeDtypeStruct((RING, m, B), jnp.float32),
        in_specs=[SMEM] + [VMEM] * 9,
        out_specs=VMEM,
        scratch_shapes=[pltpu.VMEM((rows, cols), jnp.float32)],
        compiler_params=PARAMS,
        name="multiply_last",
    )(at, *chunks, *parts, early, middle)


def pick_kernel(at_ref, *refs):
    out_ref = refs[-1]
    own = out_ref.shape[0] // (2 * RING * RING)
    starts = sum(runs(at_ref[2], at_ref[3], own), [])
    i = 0
    for ref in refs[:-1]:
        for r in range(0, ref.shape[0], own):
            out_ref[pl.ds(pl.multiple_of(starts[i], own), own), :] = ref[r:r + own, :]
            i += 1


def pick(at, chunks):
    m = sum(c.shape[0] for c in chunks)
    block = lambda rows: pl.BlockSpec((rows, B), lambda i, at: (0, at[3] * RING + at[2]))
    return pl.pallas_call(
        pick_kernel,
        out_shape=jax.ShapeDtypeStruct((m, B), jnp.float32),
        grid_spec=pltpu.PrefetchScalarGridSpec(
            num_scalar_prefetch=1,
            grid=(1,),
            in_specs=[block(c.shape[0]) for c in chunks],
            out_specs=pl.BlockSpec((m, B), lambda i, at: (0, 0)),
        ),
        compiler_params=PARAMS,
        name="pick",
    )(at, *chunks)


def gram_kernel(at_ref, r0, r1, r2, r3, jac_ref, piece_ref, turned_ref, own_ref, other_ref):
    piece = (r0[...] + r1[...]) + (r2[...] + r3[...])
    piece_ref[...] = piece
    turned_ref[...] = piece.T
    half = own_ref.shape[0]
    for out, start in ((own_ref, at_ref[0] * half), (other_ref, (1 - at_ref[0]) * half)):
        out[...] = lax.dot_general(
            piece_ref[pl.ds(pl.multiple_of(start, half), half), :],
            jac_ref[...],
            (((1,), (1,)), ((), ())),
            precision=HI,
            preferred_element_type=jnp.float32,
        )


def gram(at, came, jac):
    m = jac.shape[0]
    shape = lambda *s: jax.ShapeDtypeStruct(s, jnp.float32)
    return pl.pallas_call(
        gram_kernel,
        out_shape=(shape(m, B), shape(B, m), shape(m // 2, m), shape(m // 2, m)),
        in_specs=[SMEM] + [VMEM] * 5,
        out_specs=(VMEM,) * 4,
        compiler_params=PARAMS,
        name="gram",
    )(at, *came, jac)


def final_kernel(at_ref, neg_ref, innov_ref, p0, p1, p2, p3, rows_ref, cov_ref, new_ref, delta_ref, yh, yl, u):
    @pl.when(pl.program_id(0) == 0)
    def _():
        neg = neg_ref[...]
        for j, piece in enumerate((p0, p1, p2, p3)):
            place = lax.rem(at_ref[1] + (RING - j), RING)
            at = pl.ds(pl.multiple_of(place * B, B), B)
            yh[:, at], yl[:, at] = split(dot6(neg, piece[...]))
        u[...] = jnp.broadcast_to(-jnp.sum(neg * innov_ref[...], axis=0, keepdims=True), u.shape)

    for b in range(RING):
        at = slice(b * B, b * B + B)
        rows = rows_ref[b, 0]
        high, low = split(rows)
        change = mul(high, yh[...]) + (mul(high, yl[...]) + mul(low, yh[...]))
        new_ref[at, :] = (cov_ref[at, :] + change) * (1 / 0.98)
        delta = lax.dot_general(
            u[...], rows, (((1,), (1,)), ((), ())), precision=HI, preferred_element_type=jnp.float32
        )
        delta_ref[0, :, at] = delta[0:1, :]


def finish(at, neg, innovation, pieces, prod_rows, covariance):
    m = neg.shape[0]
    rows_dev, cols_dev = covariance.shape
    rows = rows_dev // RING
    whole = lambda *shape: pl.BlockSpec(shape, lambda i: (0,) * len(shape))
    new, delta = pl.pallas_call(
        final_kernel,
        grid=(RING,),
        out_shape=(
            jax.ShapeDtypeStruct((rows_dev, cols_dev), jnp.float32),
            jax.ShapeDtypeStruct((RING, 1, rows), jnp.float32),
        ),
        in_specs=[
            SMEM,
            whole(m, m),
            whole(m, 1),
            *[whole(m, B)] * 4,
            pl.BlockSpec((RING, 1, B, m), lambda i: (0, i, 0, 0)),
            pl.BlockSpec((rows, cols_dev), lambda i: (i, 0)),
        ],
        out_specs=(
            pl.BlockSpec((rows, cols_dev), lambda i: (i, 0)),
            pl.BlockSpec((1, 1, rows), lambda i: (i, 0, 0)),
        ),
        scratch_shapes=[
            pltpu.VMEM((m, cols_dev), jnp.bfloat16),
            pltpu.VMEM((m, cols_dev), jnp.bfloat16),
            pltpu.VMEM((8, m), jnp.float32),
        ],
        compiler_params=PARAMS,
        name="finish",
    )(at, neg, innovation, *pieces, prod_rows.reshape(RING, RING, B, m), covariance)
    return delta.reshape(rows_dev), new


def exchange(value, axes):
    return lax.all_to_all(value, axes, split_axis=0, concat_axis=0, tiled=True)


def shifted(value, axis, by):
    if axis == "row":
        return lax.ppermute(value, "row", [(i, (i + by) % RING) for i in range(RING)])
    spots = [(y, x) for y in range(RING) for x in range(RING)]
    if axis == "x":
        perm = [(y * RING + x, y * RING + (x + by) % RING) for y, x in spots]
    else:
        perm = [(y * RING + x, (y + by) % RING * RING + x) for y, x in spots]
    return lax.ppermute(value, "col", perm)


def tie(*values):
    return lax.optimization_barrier(values)


def both_ways(first, second, axes):
    near = tie(*[shifted(v, axis, by) for v, axis in zip((first, second), axes) for by in (1, -1)])
    h = first.shape[0] // 2
    far = [
        shifted(near[0][:h], axes[0], 1),
        shifted(near[1][h:], axes[0], -1),
        shifted(near[2][:h], axes[1], 1),
        shifted(near[3][h:], axes[1], -1),
    ]
    return near, far


def per_device(jacobian, covariance, noise, innovation):
    m = noise.shape[0]
    mine = jacobian.shape[0]
    rows_dev, cols_dev = covariance.shape
    g, z, col = lax.axis_index("grp"), lax.axis_index("row"), lax.axis_index("col")
    at = jnp.stack([g, z, col // RING, lax.rem(col, RING)]).astype(jnp.int32)
    reorder = lambda v: v.reshape(2, 4, 16, mine).transpose(0, 2, 1, 3).reshape(m)
    noise, innovation = reorder(noise), reorder(innovation)

    sent = jacobian.reshape(mine, 8, rows_dev).transpose(1, 0, 2)
    got = exchange(sent, ("grp", "row")).reshape(8 * mine, rows_dev)
    parts = split_array(covariance)
    half = 4 * mine
    a, b = got[:half], got[half:]
    near, far = both_ways(a, b, ("x", "y"))
    far = tie(*far)
    a4 = jnp.concatenate([a, near[0], near[1], far[0], far[1]], axis=0)
    b4 = jnp.concatenate([b, near[2], near[3], far[2], far[3]], axis=0)
    a4, b4 = tie(a4, b4)
    near, far = both_ways(a4, b4, ("y", "x"))
    early = multiply([a4, b4], parts)
    middle = multiply(near, parts)
    out = multiply_last(at, far, parts, early, middle)

    spots = [(a, b, x) for a in range(RING) for b in range(RING) for x in range(RING)]
    number = lambda a, b, x: (a * RING + b) * RING + x
    came = []
    for j in range(RING):
        perm = [(number(a, b, x), number(b, (a + j) % RING, x)) for a, b, x in spots]
        came.append(lax.ppermute(out[j], ("row", "col"), perm))
    jac = pick(at, [a4, b4, *near, *far])
    piece, turned, own, other = gram(at, came, jac)
    prod_rows = lax.all_gather(turned, "col", axis=0)

    swap = [(0, 1), (1, 0)]
    h = m // 2
    own = own + lax.ppermute(other, "grp", swap)
    perm = [(number(a, b, x), number(b, a, x)) for a, b, x in spots]
    home = lax.ppermute(piece, ("row", "col"), perm)
    summed = exchange(own.reshape(64, h // 64, m), ("row", "col"))
    share = jnp.sum(summed, axis=0, keepdims=True)
    own = exchange(jnp.broadcast_to(share, (64, h // 64, m)), ("row", "col")).reshape(h, m)
    own, home = tie(own, home)
    other = lax.ppermute(own, "grp", swap)
    pieces = [home] + [shifted(home, "row", d) for d in (1, 2, 3)]
    neg = negative_inverse(at, own, other, noise.reshape(1, m))
    return finish(at, neg, innovation.reshape(m, 1), pieces, prod_rows, covariance)


def solution(mesh):
    in_specs = (P(("grp", "row", "col"), None), P(("grp", "row"), "col"), P(), P())
    out_specs = (P(("grp", "row")), P(("grp", "row"), "col"))
    return jax.shard_map(
        per_device, mesh=mesh, in_specs=in_specs, out_specs=out_specs, check_vma=False
    )
```

```python
import functools

import jax
import jax.numpy as jnp
from jax import lax
from jax.experimental import pallas as pl
from jax.experimental.pallas import tpu as pltpu
from jax.sharding import PartitionSpec as P

HI = lax.Precision.HIGHEST
B = 128
Q = 8
RING = 4
SHIFT = (0, -1, 1, 2)


def dot6(a, b):
    return jnp.dot(a, b, precision=HI, preferred_element_type=jnp.float32)


def sweep_block(a):
    n = B // Q
    rows = [a[Q * i:Q * i + Q, :] for i in range(n)]
    lane = lax.broadcasted_iota(jnp.int32, (Q, B), 1)
    sub = lax.broadcasted_iota(jnp.int32, (Q, B), 0)
    for p in range(n):
        r = rows[p]
        cols = [jnp.broadcast_to(r[:, Q * p + j:Q * p + j + 1], (Q, B)) for j in range(Q)]
        for k in range(Q):
            inv = 1.0 / jnp.broadcast_to(cols[k][k:k + 1, :], (Q, B))
            scaled = cols[k] * inv
            new = []
            for j in range(Q):
                if j == k:
                    new.append(jnp.where(sub == k, -inv, scaled))
                else:
                    row = jnp.broadcast_to(cols[j][k:k + 1, :], (Q, B))
                    new.append(jnp.where(sub == k, row * inv, cols[j] - scaled * row))
            row = jnp.broadcast_to(r[k:k + 1, :], (Q, B))
            r = jnp.where(sub == k, row * inv, r - scaled * row)
            cols = new
        for j in range(Q):
            r = jnp.where(lane == Q * p + j, cols[j], r)
        inside = (lane >= Q * p) & (lane < Q * p + Q)
        splat = [jnp.broadcast_to(r[j:j + 1, :], (Q, B)) for j in range(Q)]
        for b in [(p + 1 + i) % n for i in range(n - 1)]:
            old = rows[b]
            acc = jnp.where(inside, 0.0, old)
            for j in range(Q):
                acc = acc - jnp.broadcast_to(old[:, Q * p + j:Q * p + j + 1], (Q, B)) * splat[j]
            rows[b] = acc
        rows[p] = r
    return jnp.concatenate(rows, axis=0)


def inverse_kernel(at_ref, own_ref, other_ref, noise_ref, innov_ref, out_ref, u_ref):
    m = out_ref.shape[0]
    half = m // 2
    n = m // B
    g = at_ref[0]

    def system():
        for source, start in ((own_ref, g * half), (other_ref, (1 - g) * half)):
            row_id = lax.broadcasted_iota(jnp.int32, (half, m), 0) + start
            col_id = lax.broadcasted_iota(jnp.int32, (half, m), 1)
            at = pl.ds(pl.multiple_of(start, half), half)
            yield at, row_id == col_id, source[...] + jnp.where(row_id == col_id, noise_ref[...], 0.0)

    for at, _, value in system():
        out_ref[at, :] = value

    def step(k, carry):
        at = pl.ds(pl.multiple_of(k * B, B), B)
        neg = sweep_block(out_ref[at, at])
        strip = out_ref[at, :]
        left = out_ref[:, at]
        col = lax.broadcasted_iota(jnp.int32, (B, m), 1)
        here = (col >= k * B) & (col < k * B + B)
        t = jnp.where(here, jnp.concatenate([neg] * n, axis=1), -dot6(neg, strip))
        big = lax.broadcasted_iota(jnp.int32, (m, m), 1)
        keep = jnp.where((big >= k * B) & (big < k * B + B), 0.0, out_ref[...])
        out_ref[...] = keep - dot6(left, t)
        out_ref[at, :] = t
        return carry

    lax.fori_loop(0, n, step, 0)

    def solve(row):
        total = jnp.zeros((1, m), jnp.float32)
        for at, diagonal, _ in system():
            column = jnp.sum(jnp.where(diagonal, row, 0.0), axis=1, keepdims=True)
            total = total - jnp.sum(out_ref[at, :] * column, axis=0, keepdims=True)
        return total

    first = solve(innov_ref[...])
    rest = innov_ref[...]
    for _, diagonal, value in system():
        column = jnp.sum(jnp.where(diagonal, first, 0.0), axis=1, keepdims=True)
        rest = rest - jnp.sum(value * column, axis=0, keepdims=True)
    u_ref[...] = first + solve(rest)


VMEM = pl.BlockSpec(memory_space=pltpu.VMEM)
SMEM = pl.BlockSpec(memory_space=pltpu.SMEM)
PARAMS = pltpu.CompilerParams(vmem_limit_bytes=20 * 2**20)


def negative_inverse(at, own, other, noise, innovation):
    m = noise.shape[1]
    return pl.pallas_call(
        inverse_kernel,
        out_shape=(jax.ShapeDtypeStruct((m, m), jnp.float32), jax.ShapeDtypeStruct((1, m), jnp.float32)),
        in_specs=[SMEM] + [VMEM] * 4,
        out_specs=(VMEM, VMEM),
        compiler_params=pltpu.CompilerParams(vmem_limit_bytes=16 * 2**20),
        cost_estimate=pl.CostEstimate(flops=20 * 10**9, bytes_accessed=2 * 2**20, transcendentals=0),
        name="inverse",
    )(at, own, other, noise, innovation)


def split(a):
    high = a.astype(jnp.bfloat16)
    return high, (a - high.astype(jnp.float32)).astype(jnp.bfloat16)


def split3(a):
    high = a.astype(jnp.bfloat16)
    rest = a - high.astype(jnp.float32)
    return (high, *split(rest))


def mul(a, b):
    return jnp.dot(a, b, preferred_element_type=jnp.float32)


def split_kernel(a_ref, *outs):
    for out, value in zip(outs, split3(a_ref[...])):
        out[...] = value


def split_array(a):
    rows, cols = a.shape
    spec = pl.BlockSpec((rows // 4, cols), lambda i: (i, 0))
    return pl.pallas_call(
        split_kernel,
        grid=(4,),
        out_shape=(jax.ShapeDtypeStruct(a.shape, jnp.bfloat16),) * 3,
        in_specs=[spec],
        out_specs=(spec,) * 3,
        compiler_params=PARAMS,
        name="split",
    )(a)


def product(chunks, parts):
    left = jnp.concatenate([c[...] for c in chunks], axis=0)
    ph, pm, pl_ = parts
    step = 512
    total = None
    for k in range(0, left.shape[1], step):
        jh, jm, jl = split3(left[:, k:k + step])
        h, mid, low = ph[k:k + step, :], pm[k:k + step, :], pl_[k:k + step, :]
        term = mul(jh, h) + ((mul(jh, mid) + mul(jm, h)) + (mul(jh, low) + mul(jm, mid) + mul(jl, h)))
        total = term if total is None else total + term
    return total


def product_kernel(n, *refs):
    refs[n + 3][...] = product(refs[:n], refs[n:n + 3])


def multiply(chunks, parts):
    rows = sum(c.shape[0] for c in chunks)
    cols = parts[0].shape[1]
    work = 12 * rows * cols * parts[0].shape[0]
    return pl.pallas_call(
        functools.partial(product_kernel, len(chunks)),
        out_shape=jax.ShapeDtypeStruct((rows, cols), jnp.float32),
        in_specs=[VMEM] * (len(chunks) + 3),
        out_specs=VMEM,
        compiler_params=PARAMS,
        cost_estimate=pl.CostEstimate(flops=work, bytes_accessed=8 * 2**20, transcendentals=0),
        name="multiply",
    )(*chunks, *parts)


def runs(y, x, own):
    def start(half, dy, dx):
        spot = lax.rem(y + (dy + RING), RING) * RING + lax.rem(x + (dx + RING), RING)
        return (half * RING * RING + spot) * own

    first = lambda step: [start(0, SHIFT[step], d) for d in SHIFT]
    second = lambda step: [start(1, d, SHIFT[step]) for d in SHIFT]
    early = first(0) + second(0)
    middle = first(1) + first(2) + second(1) + second(2)
    late = first(3) + second(3)
    return early, middle, late


def last_kernel(at_ref, c0, c1, c2, c3, ph, pm, pl_, early_ref, middle_ref, out_ref, late_ref):
    late_ref[...] = product((c0, c1, c2, c3), (ph, pm, pl_))
    own = out_ref.shape[1] // (2 * RING * RING)
    z = at_ref[1]
    for ref, starts in zip((early_ref, middle_ref, late_ref), runs(at_ref[2], at_ref[3], own)):
        for i, start in enumerate(starts):
            rows = pl.ds(pl.multiple_of(start, own), own)
            for j in range(RING):
                lanes = pl.ds(pl.multiple_of(lax.rem(z + j, RING) * B, B), B)
                out_ref[j, rows, :] = ref[i * own:(i + 1) * own, lanes]


def multiply_last(at, chunks, parts, early, middle):
    rows = sum(c.shape[0] for c in chunks)
    cols = parts[0].shape[1]
    m = rows + early.shape[0] + middle.shape[0]
    return pl.pallas_call(
        last_kernel,
        out_shape=jax.ShapeDtypeStruct((RING, m, B), jnp.float32),
        in_specs=[SMEM] + [VMEM] * 9,
        out_specs=VMEM,
        scratch_shapes=[pltpu.VMEM((rows, cols), jnp.float32)],
        compiler_params=PARAMS,
        name="multiply_last",
    )(at, *chunks, *parts, early, middle)


def pick_kernel(at_ref, *refs):
    out_ref = refs[-1]
    own = out_ref.shape[0] // (2 * RING * RING)
    starts = sum(runs(at_ref[2], at_ref[3], own), [])
    i = 0
    for ref in refs[:-1]:
        for r in range(0, ref.shape[0], own):
            out_ref[pl.ds(pl.multiple_of(starts[i], own), own), :] = ref[r:r + own, :]
            i += 1


def pick(at, chunks):
    m = sum(c.shape[0] for c in chunks)
    block = lambda rows: pl.BlockSpec((rows, B), lambda i, at: (0, at[3] * RING + at[2]))
    return pl.pallas_call(
        pick_kernel,
        out_shape=jax.ShapeDtypeStruct((m, B), jnp.float32),
        grid_spec=pltpu.PrefetchScalarGridSpec(
            num_scalar_prefetch=1,
            grid=(1,),
            in_specs=[block(c.shape[0]) for c in chunks],
            out_specs=pl.BlockSpec((m, B), lambda i, at: (0, 0)),
        ),
        compiler_params=PARAMS,
        name="pick",
    )(at, *chunks)


def gram_kernel(at_ref, r0, r1, r2, r3, jac_ref, piece_ref, turned_ref, own_ref, other_ref):
    piece = (r0[...] + r1[...]) + (r2[...] + r3[...])
    piece_ref[...] = piece
    turned_ref[...] = piece.T
    half = own_ref.shape[0]
    for out, start in ((own_ref, at_ref[0] * half), (other_ref, (1 - at_ref[0]) * half)):
        out[...] = lax.dot_general(
            piece_ref[pl.ds(pl.multiple_of(start, half), half), :],
            jac_ref[...],
            (((1,), (1,)), ((), ())),
            precision=HI,
            preferred_element_type=jnp.float32,
        )


def gram(at, came, jac):
    m = jac.shape[0]
    shape = lambda *s: jax.ShapeDtypeStruct(s, jnp.float32)
    return pl.pallas_call(
        gram_kernel,
        out_shape=(shape(m, B), shape(B, m), shape(m // 2, m), shape(m // 2, m)),
        in_specs=[SMEM] + [VMEM] * 5,
        out_specs=(VMEM,) * 4,
        compiler_params=PARAMS,
        name="gram",
    )(at, *came, jac)


def final_kernel(
    at_ref, neg_ref, u_ref, p0, p1, p2, p3, rows_hbm, cov_hbm, new_hbm, delta_ref, cols, yh, yl, rows_ref, cov_ref, new_ref, sems
):
    count = cov_ref.shape[0]
    size = cov_ref.shape[1]
    block = lambda i: pl.ds(i * size, size)
    get_rows = [pltpu.make_async_copy(rows_hbm.at[:, i], rows_ref.at[i], sems.at[0, i]) for i in range(count)]
    get_cov = [pltpu.make_async_copy(cov_hbm.at[block(i)], cov_ref.at[i], sems.at[1, i]) for i in range(count)]
    put_new = [pltpu.make_async_copy(new_ref.at[i], new_hbm.at[block(i)], sems.at[2, i]) for i in range(count)]
    for i in range(count):
        get_rows[i].start()
        get_cov[i].start()
    for j, piece in enumerate((p0, p1, p2, p3)):
        place = lax.rem(at_ref[1] + (RING - j), RING)
        cols[:, pl.ds(pl.multiple_of(place * B, B), B)] = piece[...]
    yh[...], yl[...] = split(dot6(neg_ref[...], cols[...]))
    for i in range(count):
        get_rows[i].wait()
        rows = rows_ref[i].reshape(size, cols.shape[0])
        high, low = split(rows)
        change = mul(high, yh[...]) + (mul(high, yl[...]) + mul(low, yh[...]))
        get_cov[i].wait()
        new_ref[i] = (cov_ref[i] + change) * (1 / 0.98)
        put_new[i].start()
        scaled = rows * u_ref[...]
        lanes = sum(scaled[:, k:k + B] for k in range(0, rows.shape[1], B))
        for b in range(0, size, B):
            delta_ref[:, i * size + b:i * size + b + B] = jnp.sum(lanes[b:b + B, :].T, axis=0, keepdims=True)
    for i in range(count):
        put_new[i].wait()


def finish(at, neg, u, pieces, prod_rows, covariance):
    m = neg.shape[0]
    rows_dev, cols_dev = covariance.shape
    rows = rows_dev // RING
    hbm = pl.BlockSpec(memory_space=pltpu.HBM)
    new, delta = pl.pallas_call(
        final_kernel,
        out_shape=(
            jax.ShapeDtypeStruct((rows_dev, cols_dev), jnp.float32),
            jax.ShapeDtypeStruct((1, rows_dev), jnp.float32),
        ),
        in_specs=[SMEM] + [VMEM] * 6 + [hbm, hbm],
        out_specs=(hbm, VMEM),
        scratch_shapes=[
            pltpu.VMEM((m, cols_dev), jnp.float32),
            pltpu.VMEM((m, cols_dev), jnp.bfloat16),
            pltpu.VMEM((m, cols_dev), jnp.bfloat16),
            pltpu.VMEM((RING, RING, B, m), jnp.float32),
            pltpu.VMEM((RING, rows, cols_dev), jnp.float32),
            pltpu.VMEM((RING, rows, cols_dev), jnp.float32),
            pltpu.SemaphoreType.DMA((3, RING)),
        ],
        compiler_params=pltpu.CompilerParams(vmem_limit_bytes=50 * 2**20),
        name="finish",
    )(at, neg, u, *pieces, prod_rows.reshape(RING, RING, B, m), covariance)
    return delta.reshape(rows_dev), new


def halve_kernel(n0, n1, n2, n3, f0, f1, f2, f3):
    h = f0.shape[0]
    for near, far, start in ((n0, f0, 0), (n1, f1, h), (n2, f2, 0), (n3, f3, h)):
        far[...] = near[start:start + h, :]


def halves(near):
    rows, cols = near[0].shape
    return pl.pallas_call(
        halve_kernel,
        out_shape=(jax.ShapeDtypeStruct((rows // 2, cols), jnp.float32),) * 4,
        in_specs=[VMEM] * 4,
        out_specs=(VMEM,) * 4,
        compiler_params=PARAMS,
        name="halves",
    )(*near)


def exchange(value, axes):
    return lax.all_to_all(value, axes, split_axis=0, concat_axis=0, tiled=True)


def shifted(value, axis, by):
    if axis == "row":
        return lax.ppermute(value, "row", [(i, (i + by) % RING) for i in range(RING)])
    spots = [(y, x) for y in range(RING) for x in range(RING)]
    if axis == "x":
        perm = [(y * RING + x, y * RING + (x + by) % RING) for y, x in spots]
    else:
        perm = [(y * RING + x, (y + by) % RING * RING + x) for y, x in spots]
    return lax.ppermute(value, "col", perm)


def tie(*values):
    return lax.optimization_barrier(values)


def both_ways(first, second, axes):
    near = tie(*[shifted(v, axis, by) for v, axis in zip((first, second), axes) for by in (1, -1)])
    part = halves(near)
    far = [shifted(part[i], axes[i // 2], (1, -1)[i % 2]) for i in range(4)]
    return near, far


def per_device(jacobian, covariance, noise, innovation):
    m = noise.shape[0]
    mine = jacobian.shape[0]
    rows_dev, cols_dev = covariance.shape
    g, z, col = lax.axis_index("grp"), lax.axis_index("row"), lax.axis_index("col")
    at = jnp.stack([g, z, col // RING, lax.rem(col, RING)]).astype(jnp.int32)
    reorder = lambda v: v.reshape(2, 4, 16, mine).transpose(0, 2, 1, 3).reshape(m)
    noise, innovation = reorder(noise), reorder(innovation)

    sent = jacobian.reshape(mine, 8, rows_dev).transpose(1, 0, 2)
    got = exchange(sent, ("grp", "row")).reshape(8 * mine, rows_dev)
    parts = split_array(covariance)
    half = 4 * mine
    a, b = got[:half], got[half:]
    near, far = both_ways(a, b, ("x", "y"))
    far = tie(*far)
    a4 = jnp.concatenate([a, near[0], near[1], far[0], far[1]], axis=0)
    b4 = jnp.concatenate([b, near[2], near[3], far[2], far[3]], axis=0)
    a4, b4 = tie(a4, b4)
    near, far = both_ways(a4, b4, ("y", "x"))
    early = multiply([a4, b4], parts)
    middle = multiply(near, parts)
    out = multiply_last(at, far, parts, early, middle)

    spots = [(a, b, x) for a in range(RING) for b in range(RING) for x in range(RING)]
    number = lambda a, b, x: (a * RING + b) * RING + x
    came = []
    for j in range(RING):
        perm = [(number(a, b, x), number(b, (a + j) % RING, x)) for a, b, x in spots]
        came.append(lax.ppermute(out[j], ("row", "col"), perm))
    jac = pick(at, [a4, b4, *near, *far])
    piece, turned, own, other = gram(at, came, jac)

    swap = [(0, 1), (1, 0)]
    h = m // 2
    own = own + lax.ppermute(other, "grp", swap)
    perm = [(number(a, b, x), number(b, a, x)) for a, b, x in spots]
    home = lax.ppermute(piece, ("row", "col"), perm)
    summed = exchange(own.reshape(64, h // 64, m), ("row", "col"))
    share, turned = tie(jnp.sum(summed, axis=0, keepdims=True), turned)
    prod_rows = lax.all_gather(turned, "col", axis=0)
    own = exchange(jnp.broadcast_to(share, (64, h // 64, m)), ("row", "col")).reshape(h, m)
    own, home = tie(own, home)
    other = lax.ppermute(own, "grp", swap)
    pieces = [home] + [shifted(home, "row", d) for d in (1, 2, 3)]
    neg, u = negative_inverse(at, own, other, noise.reshape(1, m), innovation.reshape(1, m))
    return finish(at, neg, u, pieces, prod_rows, covariance)


def solution(mesh):
    in_specs = (P(("grp", "row", "col"), None), P(("grp", "row"), "col"), P(), P())
    out_specs = (P(("grp", "row")), P(("grp", "row"), "col"))
    return jax.shard_map(
        per_device, mesh=mesh, in_specs=in_specs, out_specs=out_specs, check_vma=False
    )
```

```python
import functools

import jax
import jax.numpy as jnp
from jax import lax
from jax.experimental import pallas as pl
from jax.experimental.pallas import tpu as pltpu
from jax.sharding import PartitionSpec as P

HI = lax.Precision.HIGHEST
B = 128
Q = 8
RING = 4
SHIFT = (0, -1, 1, 2)
FINAL = 46


def dot6(a, b):
    return jnp.dot(a, b, precision=HI, preferred_element_type=jnp.float32)


def sweep_block(a):
    n = B // Q
    rows = [a[Q * i:Q * i + Q, :] for i in range(n)]
    lane = lax.broadcasted_iota(jnp.int32, (Q, B), 1)
    sub = lax.broadcasted_iota(jnp.int32, (Q, B), 0)
    for p in range(n):
        r = rows[p]
        cols = [jnp.broadcast_to(r[:, Q * p + j:Q * p + j + 1], (Q, B)) for j in range(Q)]
        for k in range(Q):
            inv = 1.0 / jnp.broadcast_to(cols[k][k:k + 1, :], (Q, B))
            scaled = cols[k] * inv
            new = []
            for j in range(Q):
                if j == k:
                    new.append(jnp.where(sub == k, -inv, scaled))
                else:
                    row = jnp.broadcast_to(cols[j][k:k + 1, :], (Q, B))
                    new.append(jnp.where(sub == k, row * inv, cols[j] - scaled * row))
            row = jnp.broadcast_to(r[k:k + 1, :], (Q, B))
            r = jnp.where(sub == k, row * inv, r - scaled * row)
            cols = new
        for j in range(Q):
            r = jnp.where(lane == Q * p + j, cols[j], r)
        inside = (lane >= Q * p) & (lane < Q * p + Q)
        splat = [jnp.broadcast_to(r[j:j + 1, :], (Q, B)) for j in range(Q)]
        for b in [(p + 1 + i) % n for i in range(n - 1)]:
            old = rows[b]
            acc = jnp.where(inside, 0.0, old)
            for j in range(Q):
                acc = acc - jnp.broadcast_to(old[:, Q * p + j:Q * p + j + 1], (Q, B)) * splat[j]
            rows[b] = acc
        rows[p] = r
    return jnp.concatenate(rows, axis=0)


def sweep(out_ref, k):
    m = out_ref.shape[0]
    at = pl.ds(pl.multiple_of(k * B, B), B)
    neg = sweep_block(out_ref[at, at])
    strip = out_ref[at, :]
    left = out_ref[:, at]
    col = lax.broadcasted_iota(jnp.int32, (B, m), 1)
    here = (col >= k * B) & (col < k * B + B)
    t = jnp.where(here, jnp.concatenate([neg] * (m // B), axis=1), -dot6(neg, strip))
    big = lax.broadcasted_iota(jnp.int32, (m, m), 1)
    keep = jnp.where((big >= k * B) & (big < k * B + B), 0.0, out_ref[...])
    out_ref[...] = keep - dot6(left, t)
    out_ref[at, :] = t


def system(at_ref, own_ref, other_ref, noise_ref):
    half, m = own_ref.shape
    g = at_ref[0]
    for source, start in ((own_ref, g * half), (other_ref, (1 - g) * half)):
        row_id = lax.broadcasted_iota(jnp.int32, (half, m), 0) + start
        diagonal = row_id == lax.broadcasted_iota(jnp.int32, (half, m), 1)
        at = pl.ds(pl.multiple_of(start, half), half)
        yield at, diagonal, source[...] + jnp.where(diagonal, noise_ref[...], 0.0)


def first_sweeps_kernel(at_ref, own_ref, other_ref, noise_ref, out_ref):
    for at, _, value in system(at_ref, own_ref, other_ref, noise_ref):
        out_ref[at, :] = value
    lax.fori_loop(0, out_ref.shape[0] // B // 2, lambda k, c: (sweep(out_ref, k), c)[1], 0)


def last_sweeps_kernel(at_ref, mid_ref, own_ref, other_ref, noise_ref, innov_ref, out_ref, u_ref):
    m = out_ref.shape[0]
    n = m // B
    out_ref[...] = mid_ref[...]
    lax.fori_loop(n // 2, n, lambda k, c: (sweep(out_ref, k), c)[1], 0)
    halves = lambda: system(at_ref, own_ref, other_ref, noise_ref)
    turn = lambda diagonal, row: jnp.sum(jnp.where(diagonal, row, 0.0), axis=1, keepdims=True)

    def solve(row):
        total = jnp.zeros((1, m), jnp.float32)
        for at, diagonal, _ in halves():
            total = total - jnp.sum(out_ref[at, :] * turn(diagonal, row), axis=0, keepdims=True)
        return total

    first = solve(innov_ref[...])
    rest = innov_ref[...]
    for _, diagonal, value in halves():
        rest = rest - jnp.sum(value * turn(diagonal, first), axis=0, keepdims=True)
    u_ref[...] = first + solve(rest)


VMEM = pl.BlockSpec(memory_space=pltpu.VMEM)
SMEM = pl.BlockSpec(memory_space=pltpu.SMEM)
PARAMS = pltpu.CompilerParams(vmem_limit_bytes=20 * 2**20)


SWEEPS = dict(
    compiler_params=pltpu.CompilerParams(vmem_limit_bytes=16 * 2**20),
    cost_estimate=pl.CostEstimate(flops=14 * 10**9, bytes_accessed=2 * 2**20, transcendentals=0),
)


def first_sweeps(at, own, other, noise):
    m = noise.shape[1]
    return pl.pallas_call(
        first_sweeps_kernel,
        out_shape=jax.ShapeDtypeStruct((m, m), jnp.float32),
        in_specs=[SMEM] + [VMEM] * 3,
        out_specs=VMEM,
        name="first_sweeps",
        **SWEEPS,
    )(at, own, other, noise)


def last_sweeps(at, mid, own, other, noise, innovation):
    m = noise.shape[1]
    return pl.pallas_call(
        last_sweeps_kernel,
        out_shape=(jax.ShapeDtypeStruct((m, m), jnp.float32), jax.ShapeDtypeStruct((1, m), jnp.float32)),
        in_specs=[SMEM] + [VMEM] * 5,
        out_specs=(VMEM, VMEM),
        name="last_sweeps",
        **SWEEPS,
    )(at, mid, own, other, noise, innovation)


def split(a):
    high = a.astype(jnp.bfloat16)
    return high, (a - high.astype(jnp.float32)).astype(jnp.bfloat16)


def split3(a):
    high = a.astype(jnp.bfloat16)
    rest = a - high.astype(jnp.float32)
    return (high, *split(rest))


def mul(a, b):
    return jnp.dot(a, b, preferred_element_type=jnp.float32)


def split_kernel(a_ref, *outs):
    for out, value in zip(outs, split3(a_ref[...])):
        out[...] = value


def split_array(a):
    rows, cols = a.shape
    spec = pl.BlockSpec((rows // 4, cols), lambda i: (i, 0))
    return pl.pallas_call(
        split_kernel,
        grid=(4,),
        out_shape=(jax.ShapeDtypeStruct(a.shape, jnp.bfloat16),) * 3,
        in_specs=[spec],
        out_specs=(spec,) * 3,
        compiler_params=PARAMS,
        name="split",
    )(a)


def product(chunks, parts):
    left = jnp.concatenate([c[...] for c in chunks], axis=0)
    ph, pm, pl_ = parts
    step = 512
    total = None
    for k in range(0, left.shape[1], step):
        jh, jm, jl = split3(left[:, k:k + step])
        h, mid, low = ph[k:k + step, :], pm[k:k + step, :], pl_[k:k + step, :]
        term = mul(jh, h) + ((mul(jh, mid) + mul(jm, h)) + (mul(jh, low) + mul(jm, mid) + mul(jl, h)))
        total = term if total is None else total + term
    return total


def product_kernel(n, *refs):
    refs[n + 3][...] = product(refs[:n], refs[n:n + 3])


def multiply(chunks, parts):
    rows = sum(c.shape[0] for c in chunks)
    cols = parts[0].shape[1]
    work = 12 * rows * cols * parts[0].shape[0]
    return pl.pallas_call(
        functools.partial(product_kernel, len(chunks)),
        out_shape=jax.ShapeDtypeStruct((rows, cols), jnp.float32),
        in_specs=[VMEM] * (len(chunks) + 3),
        out_specs=VMEM,
        compiler_params=PARAMS,
        cost_estimate=pl.CostEstimate(flops=work, bytes_accessed=8 * 2**20, transcendentals=0),
        name="multiply",
    )(*chunks, *parts)


def runs(y, x, place):
    def spot(half, dy, dx):
        return place(half, lax.rem(y + (dy + RING), RING), lax.rem(x + (dx + RING), RING))

    first = lambda step: [spot(0, SHIFT[step], d) for d in SHIFT]
    second = lambda step: [spot(1, d, SHIFT[step]) for d in SHIFT]
    early = first(0) + second(0)
    middle = first(1) + first(2) + second(1) + second(2)
    late = first(3) + second(3)
    return early, middle, late


def measured(own):
    return lambda half, y, x: ((half * RING + y) * RING + x) * own


def last_kernel(at_ref, c0, c1, c2, c3, ph, pm, pl_, early_ref, middle_ref, out_ref, late_ref):
    late_ref[...] = product((c0, c1, c2, c3), (ph, pm, pl_))
    own = out_ref.shape[1] // (2 * RING * RING)
    z = at_ref[1]
    for ref, starts in zip((early_ref, middle_ref, late_ref), runs(at_ref[2], at_ref[3], measured(own))):
        for i, start in enumerate(starts):
            rows = pl.ds(pl.multiple_of(start, own), own)
            for j in range(RING):
                lanes = pl.ds(pl.multiple_of(lax.rem(z + j, RING) * B, B), B)
                out_ref[j, rows, :] = ref[i * own:(i + 1) * own, lanes]


def multiply_last(at, chunks, parts, early, middle):
    rows = sum(c.shape[0] for c in chunks)
    cols = parts[0].shape[1]
    m = rows + early.shape[0] + middle.shape[0]
    return pl.pallas_call(
        last_kernel,
        out_shape=jax.ShapeDtypeStruct((RING, m, B), jnp.float32),
        in_specs=[SMEM] + [VMEM] * 9,
        out_specs=VMEM,
        scratch_shapes=[pltpu.VMEM((rows, cols), jnp.float32)],
        compiler_params=PARAMS,
        name="multiply_last",
    )(at, *chunks, *parts, early, middle)


def pick_kernel(at_ref, *refs):
    out_ref = refs[-1]
    own = out_ref.shape[0] // (2 * RING * RING)
    starts = sum(runs(at_ref[2], at_ref[3], measured(own)), [])
    i = 0
    for ref in refs[:-1]:
        for r in range(0, ref.shape[0], own):
            out_ref[pl.ds(pl.multiple_of(starts[i], own), own), :] = ref[r:r + own, :]
            i += 1


def pick(at, chunks):
    m = sum(c.shape[0] for c in chunks)
    block = lambda rows: pl.BlockSpec((rows, B), lambda i, at: (0, at[3] * RING + at[2]))
    return pl.pallas_call(
        pick_kernel,
        out_shape=jax.ShapeDtypeStruct((m, B), jnp.float32),
        grid_spec=pltpu.PrefetchScalarGridSpec(
            num_scalar_prefetch=1,
            grid=(1,),
            in_specs=[block(c.shape[0]) for c in chunks],
            out_specs=pl.BlockSpec((m, B), lambda i, at: (0, 0)),
        ),
        compiler_params=PARAMS,
        name="pick",
    )(at, *chunks)


def gram_kernel(at_ref, r0, r1, r2, r3, jac_ref, piece_ref, turned_ref, own_ref, other_ref):
    piece = (r0[...] + r1[...]) + (r2[...] + r3[...])
    piece_ref[...] = piece
    turned_ref[...] = piece.T
    half = own_ref.shape[0]
    for out, start in ((own_ref, at_ref[0] * half), (other_ref, (1 - at_ref[0]) * half)):
        out[...] = lax.dot_general(
            piece_ref[pl.ds(pl.multiple_of(start, half), half), :],
            jac_ref[...],
            (((1,), (1,)), ((), ())),
            precision=HI,
            preferred_element_type=jnp.float32,
        )


def gram(at, came, jac):
    m = jac.shape[0]
    shape = lambda *s: jax.ShapeDtypeStruct(s, jnp.float32)
    return pl.pallas_call(
        gram_kernel,
        out_shape=(shape(m, B), shape(B, m), shape(m // 2, m), shape(m // 2, m)),
        in_specs=[SMEM] + [VMEM] * 5,
        out_specs=(VMEM,) * 4,
        compiler_params=PARAMS,
        name="gram",
    )(at, *came, jac)


def final_kernel(at_ref, neg_ref, u_ref, *refs):
    pieces, chunks = refs[:RING], refs[RING:RING + 10]
    cov_hbm, new_hbm, delta_ref, cols, yh, yl, cov_ref, new_ref, get_sem, put_sem = refs[RING + 10:]
    part = B // 2
    groups = [chunks[0:2], chunks[2:4], chunks[4:6], chunks[6:10]]
    count = cov_ref.shape[1] // part
    z, y, x = at_ref[1], at_ref[2], at_ref[3]
    places = sum(runs(y, x, lambda half, y, x: (x * RING + y, half)), [])

    def copies(i):
        for j in range(count):
            n = i * count + j
            spot, half = places[n]
            hbm = pl.ds(pl.multiple_of(spot * B + half * part, part), part)
            here = pl.ds(j * part, part)
            yield (
                pltpu.make_async_copy(cov_hbm.at[hbm], cov_ref.at[i, here], get_sem.at[n]),
                pltpu.make_async_copy(new_ref.at[i, here], new_hbm.at[hbm], put_sem.at[n]),
            )

    moves = [list(copies(i)) for i in range(len(groups))]
    for group in moves:
        for get, _ in group:
            get.start()
    for j, piece in enumerate(pieces):
        place = lax.rem(z + (RING - j), RING)
        cols[:, pl.ds(pl.multiple_of(place * B, B), B)] = piece[...]
    yh[...], yl[...] = split(dot6(neg_ref[...], cols[...]))
    for i, group in enumerate(groups):
        rows = jnp.concatenate([c[...] for c in group], axis=0)
        high, low = split(rows)
        change = mul(high, yh[...]) + (mul(high, yl[...]) + mul(low, yh[...]))
        for get, _ in moves[i]:
            get.wait()
        new_ref[i] = (cov_ref[i] + change) * (1 / 0.98)
        for _, put in moves[i]:
            put.start()
        scaled = rows * u_ref[...]
        lanes = sum(scaled[:, k:k + B] for k in range(0, rows.shape[1], B))
        for j in range(count):
            spot, half = places[i * count + j]
            value = jnp.sum(lanes[j * part:j * part + part, :].T, axis=0, keepdims=True)
            delta_ref[pl.ds(spot, 1), half * part:half * part + part] = value
    for group in moves:
        for _, put in group:
            put.wait()


def finish(at, neg, u, pieces, chunks, covariance):
    m = neg.shape[0]
    rows_dev, cols_dev = covariance.shape
    rows = rows_dev // RING
    hbm = pl.BlockSpec(memory_space=pltpu.HBM)
    new, delta = pl.pallas_call(
        final_kernel,
        out_shape=(
            jax.ShapeDtypeStruct((rows_dev, cols_dev), jnp.float32),
            jax.ShapeDtypeStruct((rows_dev // B, B), jnp.float32),
        ),
        in_specs=[SMEM] + [VMEM] * (2 + RING + 10) + [hbm],
        out_specs=(hbm, VMEM),
        scratch_shapes=[
            pltpu.VMEM((m, cols_dev), jnp.float32),
            pltpu.VMEM((m, cols_dev), jnp.bfloat16),
            pltpu.VMEM((m, cols_dev), jnp.bfloat16),
            pltpu.VMEM((RING, rows, cols_dev), jnp.float32),
            pltpu.VMEM((RING, rows, cols_dev), jnp.float32),
            pltpu.SemaphoreType.DMA((2 * rows_dev // B,)),
            pltpu.SemaphoreType.DMA((2 * rows_dev // B,)),
        ],
        compiler_params=pltpu.CompilerParams(vmem_limit_bytes=FINAL * 2**20),
        name="finish",
    )(at, neg, u, *pieces, *chunks, covariance)
    return delta.reshape(rows_dev), new


def halve_kernel(n0, n1, n2, n3, f0, f1, f2, f3):
    h = f0.shape[0]
    for near, far, start in ((n0, f0, 0), (n1, f1, h), (n2, f2, 0), (n3, f3, h)):
        far[...] = near[start:start + h, :]


def halves(near):
    rows, cols = near[0].shape
    return pl.pallas_call(
        halve_kernel,
        out_shape=(jax.ShapeDtypeStruct((rows // 2, cols), jnp.float32),) * 4,
        in_specs=[VMEM] * 4,
        out_specs=(VMEM,) * 4,
        compiler_params=PARAMS,
        name="halves",
    )(*near)


def exchange(value, axes):
    return lax.all_to_all(value, axes, split_axis=0, concat_axis=0, tiled=True)


def shifted(value, axis, by):
    if axis == "row":
        return lax.ppermute(value, "row", [(i, (i + by) % RING) for i in range(RING)])
    spots = [(y, x) for y in range(RING) for x in range(RING)]
    if axis == "x":
        perm = [(y * RING + x, y * RING + (x + by) % RING) for y, x in spots]
    else:
        perm = [(y * RING + x, (y + by) % RING * RING + x) for y, x in spots]
    return lax.ppermute(value, "col", perm)


def tie(*values):
    return lax.optimization_barrier(values)


def around(first, second, axes):
    return [shifted(v, axis, by) for v, axis in zip((first, second), axes) for by in (1, -1, 2)]


def beside(first, second, axes):
    return [shifted(v, axis, by) for v, axis in zip((first, second), axes) for by in (1, -1)]


def beyond(near, axes):
    part = halves(near)
    return [shifted(part[i], axes[i // 2], (1, -1)[i % 2]) for i in range(4)]


def stack(first, second, came):
    return (
        jnp.concatenate([first, *came[:3]], axis=0),
        jnp.concatenate([second, *came[3:]], axis=0),
    )


def per_device(jacobian, covariance, noise, innovation):
    m = noise.shape[0]
    mine = jacobian.shape[0]
    rows_dev, cols_dev = covariance.shape
    g, z, col = lax.axis_index("grp"), lax.axis_index("row"), lax.axis_index("col")
    at = jnp.stack([g, z, col // RING, lax.rem(col, RING)]).astype(jnp.int32)
    reorder = lambda v: v.reshape(2, 4, 16, mine).transpose(0, 2, 1, 3).reshape(m)
    noise, innovation = reorder(noise), reorder(innovation)

    sent = jacobian.reshape(mine, 8, rows_dev).transpose(1, 0, 2)
    got = exchange(sent, ("grp", "row")).reshape(8 * mine, rows_dev)
    parts = split_array(covariance)
    half = 4 * mine
    a, b = got[:half], got[half:]
    a4, b4 = stack(a, b, tie(*around(a, b, ("x", "y"))))
    a4, b4 = tie(a4, b4)
    near = tie(*beside(a4, b4, ("y", "x")))
    far = beyond(near, ("y", "x"))
    early = multiply([a4, b4], parts)
    middle = multiply(near, parts)
    out = multiply_last(at, far, parts, early, middle)

    spots = [(a, b, x) for a in range(RING) for b in range(RING) for x in range(RING)]
    number = lambda a, b, x: (a * RING + b) * RING + x
    came = []
    for j in range(RING):
        perm = [(number(a, b, x), number(b, (a + j) % RING, x)) for a, b, x in spots]
        came.append(lax.ppermute(out[j], ("row", "col"), perm))
    jac = pick(at, [a4, b4, *near, *far])
    piece, turned, own, other = gram(at, came, jac)

    swap = [(0, 1), (1, 0)]
    h = m // 2
    a, b = turned[:B // 2], turned[B // 2:]
    own = own + lax.ppermute(other, "grp", swap)
    perm = [(number(a, b, x), number(b, a, x)) for a, b, x in spots]
    home = lax.ppermute(piece, ("row", "col"), perm)
    summed, home, *came = tie(
        exchange(own.reshape(64, h // 64, m), ("row", "col")), home, *around(a, b, ("x", "y"))
    )
    a4, b4 = stack(a, b, came)
    share = jnp.sum(summed, axis=0, keepdims=True)
    own = exchange(jnp.broadcast_to(share, (64, h // 64, m)), ("row", "col")).reshape(h, m)
    own, a4, b4, *rest = tie(own, a4, b4, *[shifted(home, "row", d) for d in (1, 2, 3)])
    other = lax.ppermute(own, "grp", swap)
    near = beside(a4, b4, ("y", "x"))
    mid = first_sweeps(at, own, other, noise.reshape(1, m))
    mid, *near = tie(mid, *near)
    far = beyond(near, ("y", "x"))
    neg, u = last_sweeps(at, mid, own, other, noise.reshape(1, m), innovation.reshape(1, m))
    neg, *far = tie(neg, *far)
    return finish(at, neg, u, [home, *rest], [a4, b4, *near, *far], covariance)


def solution(mesh):
    in_specs = (P(("grp", "row", "col"), None), P(("grp", "row"), "col"), P(), P())
    out_specs = (P(("grp", "row")), P(("grp", "row"), "col"))
    return jax.shard_map(
        per_device, mesh=mesh, in_specs=in_specs, out_specs=out_specs, check_vma=False
    )
```

```python
import functools

import jax
import jax.numpy as jnp
from jax import lax
from jax.experimental import pallas as pl
from jax.experimental.pallas import tpu as pltpu
from jax.sharding import PartitionSpec as P

HI = lax.Precision.HIGHEST
B = 128
Q = 8
RING = 4
SHIFT = (0, -1, 1, 2)
FINAL = 46


def dot6(a, b):
    return jnp.dot(a, b, precision=HI, preferred_element_type=jnp.float32)


def sweep_block(a):
    n = B // Q
    rows = [a[Q * i:Q * i + Q, :] for i in range(n)]
    lane = lax.broadcasted_iota(jnp.int32, (Q, B), 1)
    sub = lax.broadcasted_iota(jnp.int32, (Q, B), 0)
    for p in range(n):
        r = rows[p]
        cols = [jnp.broadcast_to(r[:, Q * p + j:Q * p + j + 1], (Q, B)) for j in range(Q)]
        for k in range(Q):
            inv = 1.0 / jnp.broadcast_to(cols[k][k:k + 1, :], (Q, B))
            scaled = cols[k] * inv
            new = []
            for j in range(Q):
                if j == k:
                    new.append(jnp.where(sub == k, -inv, scaled))
                else:
                    row = jnp.broadcast_to(cols[j][k:k + 1, :], (Q, B))
                    new.append(jnp.where(sub == k, row * inv, cols[j] - scaled * row))
            row = jnp.broadcast_to(r[k:k + 1, :], (Q, B))
            r = jnp.where(sub == k, row * inv, r - scaled * row)
            cols = new
        for j in range(Q):
            r = jnp.where(lane == Q * p + j, cols[j], r)
        inside = (lane >= Q * p) & (lane < Q * p + Q)
        splat = [jnp.broadcast_to(r[j:j + 1, :], (Q, B)) for j in range(Q)]
        for b in [(p + 1 + i) % n for i in range(n - 1)]:
            old = rows[b]
            acc = jnp.where(inside, 0.0, old)
            for j in range(Q):
                acc = acc - jnp.broadcast_to(old[:, Q * p + j:Q * p + j + 1], (Q, B)) * splat[j]
            rows[b] = acc
        rows[p] = r
    return jnp.concatenate(rows, axis=0)


def sweep(out_ref, k):
    m = out_ref.shape[0]
    at = pl.ds(pl.multiple_of(k * B, B), B)
    neg = sweep_block(out_ref[at, at])
    strip = out_ref[at, :]
    left = out_ref[:, at]
    col = lax.broadcasted_iota(jnp.int32, (B, m), 1)
    here = (col >= k * B) & (col < k * B + B)
    t = jnp.where(here, jnp.concatenate([neg] * (m // B), axis=1), -dot6(neg, strip))
    big = lax.broadcasted_iota(jnp.int32, (m, m), 1)
    keep = jnp.where((big >= k * B) & (big < k * B + B), 0.0, out_ref[...])
    out_ref[...] = keep - dot6(left, t)
    out_ref[at, :] = t


def inverse_kernel(at_ref, own_ref, other_ref, noise_ref, innov_ref, out_ref, u_ref, s_ref):
    m = out_ref.shape[0]
    n = m // B
    g, z = at_ref[0], at_ref[1]
    for source, half in ((own_ref, g), (other_ref, 1 - g)):
        lanes = pl.ds(pl.multiple_of(half * (m // 2), m // 2), m // 2)
        for d in range(RING):
            rows = pl.ds(pl.multiple_of(lax.rem(z + (RING - d), RING) * B, B), B)
            s_ref[rows, lanes] = source[d * B:d * B + B, :]
    diagonal = lax.broadcasted_iota(jnp.int32, (m, m), 0) == lax.broadcasted_iota(jnp.int32, (m, m), 1)
    s_ref[...] = s_ref[...] + jnp.where(diagonal, noise_ref[...], 0.0)
    out_ref[...] = s_ref[...]
    lax.fori_loop(0, n, lambda k, c: (sweep(out_ref, k), c)[1], 0)

    def apply(matrix_ref, row):
        column = jnp.sum(jnp.where(diagonal, row, 0.0), axis=1, keepdims=True)
        return jnp.sum(matrix_ref[...] * column, axis=0, keepdims=True)

    first = -apply(out_ref, innov_ref[...])
    rest = innov_ref[...] - apply(s_ref, first)
    u_ref[...] = first - apply(out_ref, rest)


VMEM = pl.BlockSpec(memory_space=pltpu.VMEM)
SMEM = pl.BlockSpec(memory_space=pltpu.SMEM)
PARAMS = pltpu.CompilerParams(vmem_limit_bytes=20 * 2**20)


def negative_inverse(at, own, other, noise, innovation):
    m = noise.shape[1]
    return pl.pallas_call(
        inverse_kernel,
        out_shape=(jax.ShapeDtypeStruct((m, m), jnp.float32), jax.ShapeDtypeStruct((1, m), jnp.float32)),
        in_specs=[SMEM] + [VMEM] * 4,
        out_specs=(VMEM, VMEM),
        scratch_shapes=[pltpu.VMEM((m, m), jnp.float32)],
        compiler_params=pltpu.CompilerParams(vmem_limit_bytes=16 * 2**20),
        cost_estimate=pl.CostEstimate(flops=25 * 10**9, bytes_accessed=2 * 2**20, transcendentals=0),
        name="inverse",
    )(at, own, other, noise, innovation)


def split(a):
    high = a.astype(jnp.bfloat16)
    return high, (a - high.astype(jnp.float32)).astype(jnp.bfloat16)


def split3(a):
    high = a.astype(jnp.bfloat16)
    rest = a - high.astype(jnp.float32)
    return (high, *split(rest))


def mul(a, b):
    return jnp.dot(a, b, preferred_element_type=jnp.float32)


def split_kernel(a_ref, *outs):
    for out, value in zip(outs, split3(a_ref[...])):
        out[...] = value


def split_array(a):
    rows, cols = a.shape
    spec = pl.BlockSpec((rows // 4, cols), lambda i: (i, 0))
    return pl.pallas_call(
        split_kernel,
        grid=(4,),
        out_shape=(jax.ShapeDtypeStruct(a.shape, jnp.bfloat16),) * 3,
        in_specs=[spec],
        out_specs=(spec,) * 3,
        compiler_params=PARAMS,
        name="split",
    )(a)


def product(chunks, parts):
    rows = sum(c.shape[0] for c in chunks)
    depth, cols = parts[0].shape
    step = 512

    def add(k, total):
        at = pl.ds(pl.multiple_of(k * step, step), step)
        jh, jm, jl = split3(jnp.concatenate([c[:, at] for c in chunks], axis=0))
        h, mid, low = [p[at, :] for p in parts]
        return total + mul(jh, h) + ((mul(jh, mid) + mul(jm, h)) + (mul(jh, low) + mul(jm, mid) + mul(jl, h)))

    return lax.fori_loop(0, depth // step, add, jnp.zeros((rows, cols), jnp.float32))


def product_kernel(n, *refs):
    refs[n + 3][...] = product(refs[:n], refs[n:n + 3])


def multiply(chunks, parts):
    rows = sum(c.shape[0] for c in chunks)
    cols = parts[0].shape[1]
    work = 12 * rows * cols * parts[0].shape[0]
    return pl.pallas_call(
        functools.partial(product_kernel, len(chunks)),
        out_shape=jax.ShapeDtypeStruct((rows, cols), jnp.float32),
        in_specs=[VMEM] * (len(chunks) + 3),
        out_specs=VMEM,
        compiler_params=PARAMS,
        cost_estimate=pl.CostEstimate(flops=work, bytes_accessed=8 * 2**20, transcendentals=0),
        name="multiply",
    )(*chunks, *parts)


def runs(y, x, place):
    def spot(half, dy, dx):
        return place(half, lax.rem(y + (dy + RING), RING), lax.rem(x + (dx + RING), RING))

    first = lambda step: [spot(0, SHIFT[step], d) for d in SHIFT]
    second = lambda step: [spot(1, d, SHIFT[step]) for d in SHIFT]
    early = first(0) + second(0)
    middle = first(1) + second(1) + first(2) + second(2)
    late = first(3) + second(3)
    return early, middle, late


def measured(own):
    return lambda half, y, x: ((half * RING + y) * RING + x) * own


def last_kernel(at_ref, c0, c1, c2, c3, ph, pm, pl_, early_ref, middle_ref, out_ref, late_ref):
    late_ref[...] = product((c0, c1, c2, c3), (ph, pm, pl_))
    own = out_ref.shape[1] // (2 * RING * RING)
    z = at_ref[1]
    for ref, starts in zip((early_ref, middle_ref, late_ref), runs(at_ref[2], at_ref[3], measured(own))):
        for i, start in enumerate(starts):
            rows = pl.ds(pl.multiple_of(start, own), own)
            for j in range(RING):
                lanes = pl.ds(pl.multiple_of(lax.rem(z + j, RING) * B, B), B)
                out_ref[j, rows, :] = ref[i * own:(i + 1) * own, lanes]


def multiply_last(at, chunks, parts, early, middle):
    rows = sum(c.shape[0] for c in chunks)
    cols = parts[0].shape[1]
    m = rows + early.shape[0] + middle.shape[0]
    return pl.pallas_call(
        last_kernel,
        out_shape=jax.ShapeDtypeStruct((RING, m, B), jnp.float32),
        in_specs=[SMEM] + [VMEM] * 9,
        out_specs=VMEM,
        scratch_shapes=[pltpu.VMEM((rows, cols), jnp.float32)],
        compiler_params=PARAMS,
        name="multiply_last",
    )(at, *chunks, *parts, early, middle)


def collect_kernel(r0, r1, r2, r3, piece_ref, first_ref, second_ref):
    piece = (r0[...] + r1[...]) + (r2[...] + r3[...])
    piece_ref[...] = piece
    half = first_ref.shape[1]
    first_ref[...] = piece[:half, :].T
    second_ref[...] = piece[half:, :].T


def collect(came):
    m = came[0].shape[0]
    shape = lambda *s: jax.ShapeDtypeStruct(s, jnp.float32)
    return pl.pallas_call(
        collect_kernel,
        out_shape=(shape(m, B), shape(B, m // 2), shape(B, m // 2)),
        in_specs=[VMEM] * 4,
        out_specs=(VMEM,) * 3,
        compiler_params=PARAMS,
        name="collect",
    )(*came)


def blocks(y, x):
    return runs(y, x, lambda half, y, x: x * RING + y)


def system_kernel(stage, count, ready, at_ref, *refs):
    derivatives, chunks = refs[:10], refs[10:10 + count]
    before = refs[10 + count] if ready else None
    outs, (products, spots, total) = refs[10 + count + ready:-3], refs[-3:]
    size = products.shape[1]
    groups = products.shape[0]
    filled = 0
    for chunk in chunks:
        products[filled // size, filled % size:filled % size + chunk.shape[0], :] = chunk[...]
        filled += chunk.shape[0]
    for n, spot in enumerate(blocks(at_ref[2], at_ref[3])[stage]):
        spots[n] = spot
    total[...] = before[...] if ready else jnp.zeros_like(total)

    def add(t, carry):
        columns = [pl.ds(pl.multiple_of(spots[t * RING + i] * B, B), B) for i in range(RING)]
        left = jnp.concatenate(
            [jnp.concatenate([d[:, c] for d in derivatives], axis=0) for c in columns], axis=1
        )
        jh, jm, jl = split3(left)
        h, mid, low = split3(products[t])
        half = lax.rem(t, 2)
        total[half] = total[half] + (
            mul(jh, h) + ((mul(jh, mid) + mul(jm, h)) + (mul(jh, low) + mul(jm, mid) + mul(jl, h)))
        )
        return carry

    lax.fori_loop(0, groups, add, 0)
    if len(outs) == 1:
        outs[0][...] = total[...]
        return
    g = at_ref[0]
    own = total.shape[1] // (2 * RING * RING)
    starts = sum(runs(at_ref[2], at_ref[3], measured(own)), [])
    for i, start in enumerate(starts):
        rows = pl.ds(pl.multiple_of(start, own), own)
        outs[0][rows, :] = total[g, i * own:i * own + own, :]
        outs[1][rows, :] = total[1 - g, i * own:i * own + own, :]


def add_system(at, stage, derivatives, chunks, before=None):
    cols = chunks[0].shape[1]
    m = 2 * cols
    groups = sum(c.shape[0] for c in chunks) // (RING * B)
    shape = lambda *s: jax.ShapeDtypeStruct(s, jnp.float32)
    ready = [] if before is None else [before]
    return pl.pallas_call(
        functools.partial(system_kernel, stage, len(chunks), len(ready)),
        out_shape=(shape(m, cols), shape(m, cols)) if stage == 2 else shape(2, m, cols),
        in_specs=[SMEM] + [VMEM] * (10 + len(chunks) + len(ready)),
        out_specs=(VMEM, VMEM) if stage == 2 else VMEM,
        scratch_shapes=[
            pltpu.VMEM((groups, RING * B, cols), jnp.float32),
            pltpu.SMEM((groups * RING,), jnp.int32),
            pltpu.VMEM((2, m, cols), jnp.float32),
        ],
        compiler_params=PARAMS,
        cost_estimate=pl.CostEstimate(flops=groups * 2 * 10**9, bytes_accessed=8 * 2**20, transcendentals=0),
        name="add_system",
    )(at, *derivatives, *chunks, *ready)


def turn_kernel(at_ref, own_ref, came_ref, *outs):
    for j, out in enumerate(outs):
        rows = pl.ds(pl.multiple_of(lax.rem(at_ref[1] + j, RING) * B, B), B)
        out[...] = own_ref[rows, :] + came_ref[rows, :]


def turn(at, own, came):
    return pl.pallas_call(
        turn_kernel,
        out_shape=(jax.ShapeDtypeStruct((B, own.shape[1]), jnp.float32),) * RING,
        in_specs=[SMEM, VMEM, VMEM],
        out_specs=(VMEM,) * RING,
        compiler_params=PARAMS,
        name="turn",
    )(at, own, came)


def final_kernel(at_ref, neg_ref, u_ref, *refs):
    pieces, chunks = refs[:RING], refs[RING:RING + 10]
    cov_hbm, new_hbm, delta_ref, cols, yh, yl, rows_ref, cov_ref, new_ref, rows_sem, get_sem, put_sem = refs[RING + 10:]
    groups, size, _ = cov_ref.shape
    half = chunks[0].shape[1]
    places = sum(blocks(at_ref[2], at_ref[3]), [])
    n = 0
    for chunk in chunks:
        for r in range(0, chunk.shape[0], B):
            rows = pl.ds(pl.multiple_of(places[n] * B, B), B)
            lanes = pl.ds(n // RING % 2 * half, half)
            pltpu.make_async_copy(chunk.at[pl.ds(r, B)], rows_ref.at[rows, lanes], rows_sem).start()
            n += 1
    for i in range(groups):
        pltpu.make_async_copy(cov_hbm.at[pl.ds(i * size, size)], cov_ref.at[i], get_sem.at[i]).start()
    for j, piece in enumerate(pieces):
        place = lax.rem(at_ref[1] + (RING - j), RING)
        cols[:, pl.ds(pl.multiple_of(place * B, B), B)] = piece[...]
    yh[...], yl[...] = split(dot6(neg_ref[...], cols[...]))
    pltpu.make_async_copy(cov_hbm, rows_ref, rows_sem).wait()

    def group(i, carry):
        block = pl.ds(pl.multiple_of(i * size, size), size)
        rows = rows_ref[block, :]
        high, low = split(rows)
        change = mul(high, yh[...]) + (mul(high, yl[...]) + mul(low, yh[...]))
        pltpu.make_async_copy(cov_hbm.at[block], cov_ref.at[i], get_sem.at[i]).wait()
        new_ref[i] = (cov_ref[i] + change) * (1 / 0.98)
        pltpu.make_async_copy(new_ref.at[i], new_hbm.at[block], put_sem.at[i]).start()
        scaled = rows * u_ref[...]
        lanes = sum(scaled[:, k:k + B] for k in range(0, rows.shape[1], B))
        for b in range(size // B):
            value = jnp.sum(lanes[b * B:b * B + B, :].T, axis=0, keepdims=True)
            delta_ref[pl.ds(i * (size // B) + b, 1), :] = value
        return carry

    lax.fori_loop(0, groups, group, 0)
    for i in range(groups):
        pltpu.make_async_copy(new_ref.at[i], new_hbm.at[pl.ds(i * size, size)], put_sem.at[i]).wait()


def finish(at, neg, u, pieces, chunks, covariance):
    m = neg.shape[0]
    rows_dev, cols_dev = covariance.shape
    rows = rows_dev // RING
    hbm = pl.BlockSpec(memory_space=pltpu.HBM)
    new, delta = pl.pallas_call(
        final_kernel,
        out_shape=(
            jax.ShapeDtypeStruct((rows_dev, cols_dev), jnp.float32),
            jax.ShapeDtypeStruct((rows_dev // B, B), jnp.float32),
        ),
        in_specs=[SMEM] + [VMEM] * (2 + RING) + [pl.BlockSpec(memory_space=pl.ANY)] * 10 + [hbm],
        out_specs=(hbm, VMEM),
        scratch_shapes=[
            pltpu.VMEM((m, cols_dev), jnp.float32),
            pltpu.VMEM((m, cols_dev), jnp.bfloat16),
            pltpu.VMEM((m, cols_dev), jnp.bfloat16),
            pltpu.VMEM((rows_dev, m), jnp.float32),
            pltpu.VMEM((RING, rows, cols_dev), jnp.float32),
            pltpu.VMEM((RING, rows, cols_dev), jnp.float32),
            pltpu.SemaphoreType.DMA,
            pltpu.SemaphoreType.DMA((RING,)),
            pltpu.SemaphoreType.DMA((RING,)),
        ],
        compiler_params=pltpu.CompilerParams(vmem_limit_bytes=FINAL * 2**20),
        name="finish",
    )(at, neg, u, *pieces, *chunks, covariance)
    return delta.reshape(rows_dev), new


def halve_kernel(n0, n1, n2, n3, f0, f1, f2, f3):
    h = f0.shape[0]
    for near, far, start in ((n0, f0, 0), (n1, f1, 0), (n2, f2, h), (n3, f3, h)):
        far[...] = near[start:start + h, :]


def halves(near):
    rows, cols = near[0].shape
    return pl.pallas_call(
        halve_kernel,
        out_shape=(jax.ShapeDtypeStruct((rows // 2, cols), jnp.float32),) * 4,
        in_specs=[VMEM] * 4,
        out_specs=(VMEM,) * 4,
        compiler_params=PARAMS,
        name="halves",
    )(*near)


def exchange(value, axes):
    return lax.all_to_all(value, axes, split_axis=0, concat_axis=0, tiled=True)


def shifted(value, axis, by):
    if axis == "row":
        return lax.ppermute(value, "row", [(i, (i + by) % RING) for i in range(RING)])
    spots = [(y, x) for y in range(RING) for x in range(RING)]
    if axis == "x":
        perm = [(y * RING + x, y * RING + (x + by) % RING) for y, x in spots]
    else:
        perm = [(y * RING + x, (y + by) % RING * RING + x) for y, x in spots]
    return lax.ppermute(value, "col", perm)


def tie(*values):
    return lax.optimization_barrier(values)


def around(first, second, axes):
    return [shifted(v, axis, by) for v, axis in zip((first, second), axes) for by in (1, -1, 2)]


def beside(first, second, axes):
    return [shifted(v, axis, by) for by in (1, -1) for v, axis in zip((first, second), axes)]


def beyond(near, axes):
    part = halves(near)
    return [shifted(part[i], axes[i % 2], (1, -1)[i // 2]) for i in (0, 2, 1, 3)]


def stack(first, second, came):
    return (
        jnp.concatenate([first, *came[:3]], axis=0),
        jnp.concatenate([second, *came[3:]], axis=0),
    )


def per_device(jacobian, covariance, noise, innovation):
    m = noise.shape[0]
    mine = jacobian.shape[0]
    rows_dev, cols_dev = covariance.shape
    g, z, col = lax.axis_index("grp"), lax.axis_index("row"), lax.axis_index("col")
    at = jnp.stack([g, z, col // RING, lax.rem(col, RING)]).astype(jnp.int32)
    reorder = lambda v: v.reshape(2, 4, 16, mine).transpose(0, 2, 1, 3).reshape(m)
    noise, innovation = reorder(noise), reorder(innovation)

    sent = jacobian.reshape(mine, 8, rows_dev).transpose(1, 0, 2)
    got = exchange(sent, ("grp", "row")).reshape(8 * mine, rows_dev)
    parts = split_array(covariance)
    half = 4 * mine
    a, b = got[:half], got[half:]
    a4, b4 = stack(a, b, tie(*around(a, b, ("x", "y"))))
    a4, b4 = tie(a4, b4)
    near = tie(*beside(a4, b4, ("y", "x")))
    far = beyond(near, ("y", "x"))
    early = multiply([a4, b4], parts)
    middle = multiply(near, parts)
    out = multiply_last(at, far, parts, early, middle)

    spots = [(a, b, x) for a in range(RING) for b in range(RING) for x in range(RING)]
    number = lambda a, b, x: (a * RING + b) * RING + x
    came = []
    for j in range(RING):
        perm = [(number(a, b, x), number(b, (a + j) % RING, x)) for a, b, x in spots]
        came.append(lax.ppermute(out[j], ("row", "col"), perm))
    piece, a, b = collect(came)
    derivatives = [a4, b4, *near, *far]

    perm = [(number(a, b, x), number(b, a, x)) for a, b, x in spots]
    home = lax.ppermute(piece, ("row", "col"), perm)
    home, *came = tie(home, *around(a, b, ("x", "y")))
    a4, b4 = tie(*stack(a, b, came))
    near = tie(*beside(a4, b4, ("y", "x")))
    far = beyond(near, ("y", "x"))
    system = add_system(at, 0, derivatives, [a4, b4])
    system = add_system(at, 1, derivatives, near, system)
    own, other = add_system(at, 2, derivatives, far, system)

    swap = [(0, 1), (1, 0)]
    parts = turn(at, own, lax.ppermute(other, "grp", swap))
    share = parts[0] + sum(shifted(parts[d], "row", d) for d in (1, 2, 3))
    own = jnp.concatenate([share, *[shifted(share, "row", d) for d in (1, 2, 3)]], axis=0)
    own, home = tie(own, home)
    other = lax.ppermute(own, "grp", swap)
    pieces = [home, *[shifted(home, "row", d) for d in (1, 2, 3)]]
    neg, u = negative_inverse(at, own, other, noise.reshape(1, m), innovation.reshape(1, m))
    return finish(at, neg, u, pieces, [a4, b4, *near, *far], covariance)


def solution(mesh):
    in_specs = (P(("grp", "row", "col"), None), P(("grp", "row"), "col"), P(), P())
    out_specs = (P(("grp", "row")), P(("grp", "row"), "col"))
    return jax.shard_map(
        per_device, mesh=mesh, in_specs=in_specs, out_specs=out_specs, check_vma=False
    )
```

```python
import functools

import jax
import jax.numpy as jnp
from jax import lax
from jax.experimental import pallas as pl
from jax.experimental.pallas import tpu as pltpu
from jax.sharding import PartitionSpec as P

HI = lax.Precision.HIGHEST
B = 128
Q = 8
RING = 4
SHIFT = (0, -1, 1, 2)


def dot6(a, b):
    return jnp.dot(a, b, precision=HI, preferred_element_type=jnp.float32)


def sweep_block(a):
    n = B // Q
    rows = [a[Q * i:Q * i + Q, :] for i in range(n)]
    lane = lax.broadcasted_iota(jnp.int32, (Q, B), 1)
    sub = lax.broadcasted_iota(jnp.int32, (Q, B), 0)
    for p in range(n):
        r = rows[p]
        cols = [jnp.broadcast_to(r[:, Q * p + j:Q * p + j + 1], (Q, B)) for j in range(Q)]
        for k in range(Q):
            pivot = jnp.broadcast_to(cols[k][k:k + 1, :], (Q, B))
            inv = pl.reciprocal(pivot, approx=True)
            inv = inv * (2.0 - pivot * inv)
            scaled = cols[k] * inv
            new = []
            for j in range(Q):
                if j == k:
                    new.append(jnp.where(sub == k, -inv, scaled))
                else:
                    row = jnp.broadcast_to(cols[j][k:k + 1, :], (Q, B))
                    new.append(jnp.where(sub == k, row * inv, cols[j] - scaled * row))
            row = jnp.broadcast_to(r[k:k + 1, :], (Q, B))
            r = jnp.where(sub == k, row * inv, r - scaled * row)
            cols = new
        for j in range(Q):
            r = jnp.where(lane == Q * p + j, cols[j], r)
        inside = (lane >= Q * p) & (lane < Q * p + Q)
        splat = [jnp.broadcast_to(r[j:j + 1, :], (Q, B)) for j in range(Q)]
        for b in [(p + 1 + i) % n for i in range(n - 1)]:
            old = rows[b]
            acc = jnp.where(inside, 0.0, old)
            for j in range(Q):
                acc = acc - jnp.broadcast_to(old[:, Q * p + j:Q * p + j + 1], (Q, B)) * splat[j]
            rows[b] = acc
        rows[p] = r
    return jnp.concatenate(rows, axis=0)


def sweep_all(out_ref, diag_ref, left_ref, turn_ref):
    m = out_ref.shape[0]
    n = m // B
    place = lambda k: pl.ds(pl.multiple_of(k * B, B), B)
    diag_ref[...] = out_ref[:B, :B]
    left_ref[...] = jnp.zeros_like(left_ref)
    turn_ref[...] = jnp.zeros_like(turn_ref)

    def update(k):
        last = place(jnp.maximum(k - 1, 0))
        lane = lax.broadcasted_iota(jnp.int32, (m, m), 1)
        inside = (lane >= (k - 1) * B) & (lane < k * B)
        out_ref[...] = jnp.where(inside, 0.0, out_ref[...]) - dot6(left_ref[...], turn_ref[...])
        out_ref[last, :] = jnp.where(k > 0, turn_ref[...], out_ref[last, :])

    def step(k, carry):
        neg = sweep_block(diag_ref[...])
        update(k)
        at, after = place(k), place(jnp.minimum(k + 1, n - 1))
        lane = lax.broadcasted_iota(jnp.int32, (B, m), 1)
        here = (lane >= k * B) & (lane < k * B + B)
        turn_ref[...] = jnp.where(here, jnp.concatenate([neg] * n, axis=1), -dot6(neg, out_ref[at, :]))
        left_ref[...] = out_ref[:, at]
        diag_ref[...] = out_ref[after, after] - dot6(left_ref[after, :], turn_ref[:, after])
        return carry

    lax.fori_loop(0, n, step, 0)
    update(n)


def inverse_kernel(at_ref, own_ref, other_ref, noise_ref, innov_ref, out_ref, u_ref, s_ref, *scratch):
    m = out_ref.shape[0]
    half = m // 2
    g = at_ref[0]
    s_ref[pl.ds(pl.multiple_of(g * half, half), half), :] = own_ref[...]
    s_ref[pl.ds(pl.multiple_of((1 - g) * half, half), half), :] = other_ref[...]
    diagonal = lax.broadcasted_iota(jnp.int32, (m, m), 0) == lax.broadcasted_iota(jnp.int32, (m, m), 1)
    s_ref[...] = s_ref[...] + jnp.where(diagonal, noise_ref[...], 0.0)
    out_ref[...] = s_ref[...]
    sweep_all(out_ref, *scratch)

    def apply(matrix_ref, row):
        column = jnp.broadcast_to(row, (B, m)).T
        parts = [jnp.sum(matrix_ref[:, i:i + B] * column, axis=0, keepdims=True) for i in range(0, m, B)]
        return jnp.concatenate(parts, axis=1)

    first = -apply(out_ref, innov_ref[...])
    rest = innov_ref[...] - apply(s_ref, first)
    u_ref[...] = first - apply(out_ref, rest)


VMEM = pl.BlockSpec(memory_space=pltpu.VMEM)
SMEM = pl.BlockSpec(memory_space=pltpu.SMEM)
PARAMS = pltpu.CompilerParams(vmem_limit_bytes=20 * 2**20)


def negative_inverse(at, own, other, noise, innovation):
    m = noise.shape[1]
    return pl.pallas_call(
        inverse_kernel,
        out_shape=(jax.ShapeDtypeStruct((m, m), jnp.float32), jax.ShapeDtypeStruct((1, m), jnp.float32)),
        in_specs=[SMEM] + [VMEM] * 4,
        out_specs=(VMEM, VMEM),
        scratch_shapes=[pltpu.VMEM(s, jnp.float32) for s in ((m, m), (B, B), (m, B), (B, m))],
        compiler_params=pltpu.CompilerParams(vmem_limit_bytes=16 * 2**20),
        cost_estimate=pl.CostEstimate(flops=25 * 10**9, bytes_accessed=2 * 2**20, transcendentals=0),
        name="inverse",
    )(at, own, other, noise, innovation)


def split(a):
    high = a.astype(jnp.bfloat16)
    return high, (a - high.astype(jnp.float32)).astype(jnp.bfloat16)


def split3(a):
    high = a.astype(jnp.bfloat16)
    rest = a - high.astype(jnp.float32)
    return (high, *split(rest))


def mul(a, b):
    return jnp.dot(a, b, preferred_element_type=jnp.float32)


def split_kernel(a_ref, *outs):
    for out, value in zip(outs, split3(a_ref[...])):
        out[...] = value


def split_array(a):
    rows, cols = a.shape
    spec = pl.BlockSpec((rows // 4, cols), lambda i: (i, 0))
    return pl.pallas_call(
        split_kernel,
        grid=(4,),
        out_shape=(jax.ShapeDtypeStruct(a.shape, jnp.bfloat16),) * 3,
        in_specs=[spec],
        out_specs=(spec,) * 3,
        compiler_params=PARAMS,
        name="split",
    )(a)


def product(chunks, parts):
    left = jnp.concatenate([c[...] for c in chunks], axis=0)
    ph, pm, pl_ = parts
    step = 512
    total = None
    for k in range(0, left.shape[1], step):
        jh, jm, jl = split3(left[:, k:k + step])
        h, mid, low = ph[k:k + step, :], pm[k:k + step, :], pl_[k:k + step, :]
        term = mul(jh, h) + ((mul(jh, mid) + mul(jm, h)) + (mul(jh, low) + mul(jm, mid) + mul(jl, h)))
        total = term if total is None else total + term
    return total


def product_kernel(n, *refs):
    refs[n + 3][...] = product(refs[:n], refs[n:n + 3])


def multiply(chunks, parts):
    rows = sum(c.shape[0] for c in chunks)
    cols = parts[0].shape[1]
    work = 12 * rows * cols * parts[0].shape[0]
    return pl.pallas_call(
        functools.partial(product_kernel, len(chunks)),
        out_shape=jax.ShapeDtypeStruct((rows, cols), jnp.float32),
        in_specs=[VMEM] * (len(chunks) + 3),
        out_specs=VMEM,
        compiler_params=PARAMS,
        cost_estimate=pl.CostEstimate(flops=work, bytes_accessed=8 * 2**20, transcendentals=0),
        name="multiply",
    )(*chunks, *parts)


def runs(y, x, own):
    def start(half, dy, dx):
        spot = lax.rem(y + (dy + RING), RING) * RING + lax.rem(x + (dx + RING), RING)
        return (half * RING * RING + spot) * own

    first = lambda step: [start(0, SHIFT[step], d) for d in SHIFT]
    second = lambda step: [start(1, d, SHIFT[step]) for d in SHIFT]
    early = first(0) + second(0)
    middle = first(1) + first(2) + second(1) + second(2)
    late = first(3) + second(3)
    return early, middle, late


def last_kernel(at_ref, c0, c1, c2, c3, ph, pm, pl_, early_ref, middle_ref, out_ref, late_ref):
    late_ref[...] = product((c0, c1, c2, c3), (ph, pm, pl_))
    own = out_ref.shape[1] // (2 * RING * RING)
    z = at_ref[1]
    for ref, starts in zip((early_ref, middle_ref, late_ref), runs(at_ref[2], at_ref[3], own)):
        for i, start in enumerate(starts):
            rows = pl.ds(pl.multiple_of(start, own), own)
            for j in range(RING):
                lanes = pl.ds(pl.multiple_of(lax.rem(z + j, RING) * B, B), B)
                out_ref[j, rows, :] = ref[i * own:(i + 1) * own, lanes]


def multiply_last(at, chunks, parts, early, middle):
    rows = sum(c.shape[0] for c in chunks)
    cols = parts[0].shape[1]
    m = rows + early.shape[0] + middle.shape[0]
    return pl.pallas_call(
        last_kernel,
        out_shape=jax.ShapeDtypeStruct((RING, m, B), jnp.float32),
        in_specs=[SMEM] + [VMEM] * 9,
        out_specs=VMEM,
        scratch_shapes=[pltpu.VMEM((rows, cols), jnp.float32)],
        compiler_params=PARAMS,
        name="multiply_last",
    )(at, *chunks, *parts, early, middle)


def pick_kernel(at_ref, *refs):
    out_ref = refs[-1]
    own = out_ref.shape[0] // (2 * RING * RING)
    starts = sum(runs(at_ref[2], at_ref[3], own), [])
    i = 0
    for ref in refs[:-1]:
        for r in range(0, ref.shape[0], own):
            out_ref[pl.ds(pl.multiple_of(starts[i], own), own), :] = ref[r:r + own, :]
            i += 1


def pick(at, chunks):
    m = sum(c.shape[0] for c in chunks)
    block = lambda rows: pl.BlockSpec((rows, B), lambda i, at: (0, at[3] * RING + at[2]))
    return pl.pallas_call(
        pick_kernel,
        out_shape=jax.ShapeDtypeStruct((m, B), jnp.float32),
        grid_spec=pltpu.PrefetchScalarGridSpec(
            num_scalar_prefetch=1,
            grid=(1,),
            in_specs=[block(c.shape[0]) for c in chunks],
            out_specs=pl.BlockSpec((m, B), lambda i, at: (0, 0)),
        ),
        compiler_params=PARAMS,
        name="pick",
    )(at, *chunks)


def gram_kernel(at_ref, r0, r1, r2, r3, jac_ref, piece_ref, turned_ref, own_ref, other_ref):
    piece = (r0[...] + r1[...]) + (r2[...] + r3[...])
    piece_ref[...] = piece
    turned_ref[...] = piece.T
    half = own_ref.shape[0]
    for out, start in ((own_ref, at_ref[0] * half), (other_ref, (1 - at_ref[0]) * half)):
        out[...] = lax.dot_general(
            piece_ref[pl.ds(pl.multiple_of(start, half), half), :],
            jac_ref[...],
            (((1,), (1,)), ((), ())),
            precision=HI,
            preferred_element_type=jnp.float32,
        )


def gram(at, came, jac):
    m = jac.shape[0]
    shape = lambda *s: jax.ShapeDtypeStruct(s, jnp.float32)
    return pl.pallas_call(
        gram_kernel,
        out_shape=(shape(m, B), shape(B, m), shape(m // 2, m), shape(m // 2, m)),
        in_specs=[SMEM] + [VMEM] * 5,
        out_specs=(VMEM,) * 4,
        compiler_params=PARAMS,
        name="gram",
    )(at, *came, jac)


def final_kernel(
    at_ref, neg_ref, u_ref, p0, p1, p2, p3, rows_hbm, cov_hbm, new_hbm, delta_ref, cols, yh, yl, rows_ref, cov_ref, new_ref, sems
):
    count = cov_ref.shape[0]
    size = cov_ref.shape[1]
    block = lambda i: pl.ds(i * size, size)
    get_rows = [pltpu.make_async_copy(rows_hbm.at[:, i], rows_ref.at[i], sems.at[0, i]) for i in range(count)]
    get_cov = [pltpu.make_async_copy(cov_hbm.at[block(i)], cov_ref.at[i], sems.at[1, i]) for i in range(count)]
    put_new = [pltpu.make_async_copy(new_ref.at[i], new_hbm.at[block(i)], sems.at[2, i]) for i in range(count)]
    for i in range(count):
        get_rows[i].start()
        get_cov[i].start()
    for j, piece in enumerate((p0, p1, p2, p3)):
        place = lax.rem(at_ref[1] + (RING - j), RING)
        cols[:, pl.ds(pl.multiple_of(place * B, B), B)] = piece[...]
    yh[...], yl[...] = split(dot6(neg_ref[...], cols[...]))
    for i in range(count):
        get_rows[i].wait()
        rows = rows_ref[i].reshape(size, cols.shape[0])
        high, low = split(rows)
        change = mul(high, yh[...]) + (mul(high, yl[...]) + mul(low, yh[...]))
        get_cov[i].wait()
        new_ref[i] = (cov_ref[i] + change) * (1 / 0.98)
        put_new[i].start()
        scaled = rows * u_ref[...]
        lanes = sum(scaled[:, k:k + B] for k in range(0, rows.shape[1], B))
        for b in range(0, size, B):
            delta_ref[:, i * size + b:i * size + b + B] = jnp.sum(lanes[b:b + B, :].T, axis=0, keepdims=True)
    for i in range(count):
        put_new[i].wait()


def finish(at, neg, u, pieces, prod_rows, covariance):
    m = neg.shape[0]
    rows_dev, cols_dev = covariance.shape
    rows = rows_dev // RING
    hbm = pl.BlockSpec(memory_space=pltpu.HBM)
    new, delta = pl.pallas_call(
        final_kernel,
        out_shape=(
            jax.ShapeDtypeStruct((rows_dev, cols_dev), jnp.float32),
            jax.ShapeDtypeStruct((1, rows_dev), jnp.float32),
        ),
        in_specs=[SMEM] + [VMEM] * 6 + [hbm, hbm],
        out_specs=(hbm, VMEM),
        scratch_shapes=[
            pltpu.VMEM((m, cols_dev), jnp.float32),
            pltpu.VMEM((m, cols_dev), jnp.bfloat16),
            pltpu.VMEM((m, cols_dev), jnp.bfloat16),
            pltpu.VMEM((RING, RING, B, m), jnp.float32),
            pltpu.VMEM((RING, rows, cols_dev), jnp.float32),
            pltpu.VMEM((RING, rows, cols_dev), jnp.float32),
            pltpu.SemaphoreType.DMA((3, RING)),
        ],
        compiler_params=pltpu.CompilerParams(vmem_limit_bytes=50 * 2**20),
        name="finish",
    )(at, neg, u, *pieces, prod_rows.reshape(RING, RING, B, m), covariance)
    return delta.reshape(rows_dev), new


def halve_kernel(n0, n1, n2, n3, f0, f1, f2, f3):
    for near, far in ((n0, f0), (n1, f1), (n2, f2), (n3, f3)):
        far[...] = near[...]


def halves(near):
    rows, cols = near[0].shape
    block = lambda which: pl.BlockSpec((rows // 2, cols), lambda i: (which, 0))
    return pl.pallas_call(
        halve_kernel,
        grid=(1,),
        out_shape=(jax.ShapeDtypeStruct((rows // 2, cols), jnp.float32),) * 4,
        in_specs=[block(0), block(1), block(0), block(1)],
        out_specs=(block(0),) * 4,
        compiler_params=PARAMS,
        name="halves",
    )(*near)


def exchange(value, axes):
    return lax.all_to_all(value, axes, split_axis=0, concat_axis=0, tiled=True)


def shifted(value, axis, by):
    if axis == "row":
        return lax.ppermute(value, "row", [(i, (i + by) % RING) for i in range(RING)])
    spots = [(y, x) for y in range(RING) for x in range(RING)]
    if axis == "x":
        perm = [(y * RING + x, y * RING + (x + by) % RING) for y, x in spots]
    else:
        perm = [(y * RING + x, (y + by) % RING * RING + x) for y, x in spots]
    return lax.ppermute(value, "col", perm)


def tie(*values):
    return lax.optimization_barrier(values)


def both_ways(first, second, axes):
    near = tie(*[shifted(v, axis, by) for v, axis in zip((first, second), axes) for by in (1, -1)])
    part = halves(near)
    far = [shifted(part[i], axes[i // 2], (1, -1)[i % 2]) for i in range(4)]
    return near, far


def per_device(jacobian, covariance, noise, innovation):
    m = noise.shape[0]
    mine = jacobian.shape[0]
    rows_dev, cols_dev = covariance.shape
    g, z, col = lax.axis_index("grp"), lax.axis_index("row"), lax.axis_index("col")
    at = jnp.stack([g, z, col // RING, lax.rem(col, RING)]).astype(jnp.int32)
    reorder = lambda v: v.reshape(2, 4, 16, mine).transpose(0, 2, 1, 3).reshape(m)
    noise, innovation = reorder(noise), reorder(innovation)

    sent = jacobian.reshape(mine, 8, rows_dev).transpose(1, 0, 2)
    got = exchange(sent, ("grp", "row")).reshape(8 * mine, rows_dev)
    parts = split_array(covariance)
    half = 4 * mine
    a, b = got[:half], got[half:]
    near, far = both_ways(a, b, ("x", "y"))
    far = tie(*far)
    a4 = jnp.concatenate([a, near[0], near[1], far[0], far[1]], axis=0)
    b4 = jnp.concatenate([b, near[2], near[3], far[2], far[3]], axis=0)
    a4, b4 = tie(a4, b4)
    near, far = both_ways(a4, b4, ("y", "x"))
    early = multiply([a4, b4], parts)
    middle = multiply(near, parts)
    out = multiply_last(at, far, parts, early, middle)

    spots = [(a, b, x) for a in range(RING) for b in range(RING) for x in range(RING)]
    number = lambda a, b, x: (a * RING + b) * RING + x
    came = []
    for j in range(RING):
        perm = [(number(a, b, x), number(b, (a + j) % RING, x)) for a, b, x in spots]
        came.append(lax.ppermute(out[j], ("row", "col"), perm))
    jac = pick(at, [a4, b4, *near, *far])
    piece, turned, own, other = gram(at, came, jac)

    swap = [(0, 1), (1, 0)]
    h = m // 2
    own = own + lax.ppermute(other, "grp", swap)
    perm = [(number(a, b, x), number(b, a, x)) for a, b, x in spots]
    home = lax.ppermute(piece, ("row", "col"), perm)
    summed = exchange(own.reshape(64, h // 64, m), ("row", "col"))
    share, turned = tie(jnp.sum(summed, axis=0, keepdims=True), turned)
    prod_rows = lax.all_gather(turned, "col", axis=0)
    own = exchange(jnp.broadcast_to(share, (64, h // 64, m)), ("row", "col")).reshape(h, m)
    own, home = tie(own, home)
    other = lax.ppermute(own, "grp", swap)
    pieces = [home] + [shifted(home, "row", d) for d in (1, 2, 3)]
    neg, u = negative_inverse(at, own, other, noise.reshape(1, m), innovation.reshape(1, m))
    return finish(at, neg, u, pieces, prod_rows, covariance)


def solution(mesh):
    in_specs = (P(("grp", "row", "col"), None), P(("grp", "row"), "col"), P(), P())
    out_specs = (P(("grp", "row")), P(("grp", "row"), "col"))
    return jax.shard_map(
        per_device, mesh=mesh, in_specs=in_specs, out_specs=out_specs, check_vma=False
    )
```

```python
import functools

import jax
import jax.numpy as jnp
from jax import lax
from jax.experimental import pallas as pl
from jax.experimental.pallas import tpu as pltpu
from jax.sharding import PartitionSpec as P

HI = lax.Precision.HIGHEST
B = 128
Q = 8
RING = 4
SHIFT = (0, -1, 1, 2)


def dot6(a, b):
    return jnp.dot(a, b, precision=HI, preferred_element_type=jnp.float32)


def sweep_block(a):
    n = B // Q
    rows = [a[Q * i:Q * i + Q, :] for i in range(n)]
    lane = lax.broadcasted_iota(jnp.int32, (Q, B), 1)
    sub = lax.broadcasted_iota(jnp.int32, (Q, B), 0)
    for p in range(n):
        r = rows[p]
        cols = [jnp.broadcast_to(r[:, Q * p + j:Q * p + j + 1], (Q, B)) for j in range(Q)]
        for k in range(Q):
            pivot = jnp.broadcast_to(cols[k][k:k + 1, :], (Q, B))
            inv = pl.reciprocal(pivot, approx=True)
            inv = inv * (2.0 - pivot * inv)
            scaled = cols[k] * inv
            new = []
            for j in range(Q):
                if j == k:
                    new.append(jnp.where(sub == k, -inv, scaled))
                else:
                    row = jnp.broadcast_to(cols[j][k:k + 1, :], (Q, B))
                    new.append(jnp.where(sub == k, row * inv, cols[j] - scaled * row))
            row = jnp.broadcast_to(r[k:k + 1, :], (Q, B))
            r = jnp.where(sub == k, row * inv, r - scaled * row)
            cols = new
        for j in range(Q):
            r = jnp.where(lane == Q * p + j, cols[j], r)
        inside = (lane >= Q * p) & (lane < Q * p + Q)
        splat = [jnp.broadcast_to(r[j:j + 1, :], (Q, B)) for j in range(Q)]
        for b in [(p + 1 + i) % n for i in range(n - 1)]:
            old = rows[b]
            acc = jnp.where(inside, 0.0, old)
            for j in range(Q):
                acc = acc - jnp.broadcast_to(old[:, Q * p + j:Q * p + j + 1], (Q, B)) * splat[j]
            rows[b] = acc
        rows[p] = r
    return jnp.concatenate(rows, axis=0)


def sweep_all(out_ref, diag_ref, left_ref, turn_ref):
    m = out_ref.shape[0]
    n = m // B
    place = lambda k: pl.ds(pl.multiple_of(k * B, B), B)
    diag_ref[...] = out_ref[:B, :B]
    left_ref[...] = jnp.zeros_like(left_ref)
    turn_ref[...] = jnp.zeros_like(turn_ref)

    def update(k):
        last = place(jnp.maximum(k - 1, 0))
        lane = lax.broadcasted_iota(jnp.int32, (m, m), 1)
        inside = (lane >= (k - 1) * B) & (lane < k * B)
        out_ref[...] = jnp.where(inside, 0.0, out_ref[...]) - dot6(left_ref[...], turn_ref[...])
        out_ref[last, :] = jnp.where(k > 0, turn_ref[...], out_ref[last, :])

    def step(k, carry):
        neg = sweep_block(diag_ref[...])
        update(k)
        at, after = place(k), place(jnp.minimum(k + 1, n - 1))
        lane = lax.broadcasted_iota(jnp.int32, (B, m), 1)
        here = (lane >= k * B) & (lane < k * B + B)
        turn_ref[...] = jnp.where(here, jnp.concatenate([neg] * n, axis=1), -dot6(neg, out_ref[at, :]))
        left_ref[...] = out_ref[:, at]
        diag_ref[...] = out_ref[after, after] - dot6(left_ref[after, :], turn_ref[:, after])
        return carry

    lax.fori_loop(0, n, step, 0)
    update(n)


def inverse_kernel(at_ref, own_ref, other_ref, noise_ref, innov_ref, out_ref, u_ref, s_ref, *scratch):
    m = out_ref.shape[0]
    half = m // 2
    g = at_ref[0]
    s_ref[pl.ds(pl.multiple_of(g * half, half), half), :] = own_ref[...]
    s_ref[pl.ds(pl.multiple_of((1 - g) * half, half), half), :] = other_ref[...]
    diagonal = lax.broadcasted_iota(jnp.int32, (m, m), 0) == lax.broadcasted_iota(jnp.int32, (m, m), 1)
    s_ref[...] = s_ref[...] + jnp.where(diagonal, noise_ref[...], 0.0)
    out_ref[...] = s_ref[...]
    sweep_all(out_ref, *scratch)

    def apply(matrix_ref, row):
        column = jnp.broadcast_to(row, (B, m)).T
        parts = [jnp.sum(matrix_ref[:, i:i + B] * column, axis=0, keepdims=True) for i in range(0, m, B)]
        return jnp.concatenate(parts, axis=1)

    first = -apply(out_ref, innov_ref[...])
    rest = innov_ref[...] - apply(s_ref, first)
    u_ref[...] = first - apply(out_ref, rest)


VMEM = pl.BlockSpec(memory_space=pltpu.VMEM)
SMEM = pl.BlockSpec(memory_space=pltpu.SMEM)
PARAMS = pltpu.CompilerParams(vmem_limit_bytes=20 * 2**20)


def negative_inverse(at, own, other, noise, innovation):
    m = noise.shape[1]
    return pl.pallas_call(
        inverse_kernel,
        out_shape=(jax.ShapeDtypeStruct((m, m), jnp.float32), jax.ShapeDtypeStruct((1, m), jnp.float32)),
        in_specs=[SMEM] + [VMEM] * 4,
        out_specs=(VMEM, VMEM),
        scratch_shapes=[pltpu.VMEM(s, jnp.float32) for s in ((m, m), (B, B), (m, B), (B, m))],
        compiler_params=pltpu.CompilerParams(vmem_limit_bytes=16 * 2**20),
        cost_estimate=pl.CostEstimate(flops=25 * 10**9, bytes_accessed=2 * 2**20, transcendentals=0),
        name="inverse",
    )(at, own, other, noise, innovation)


def split(a):
    high = a.astype(jnp.bfloat16)
    return high, (a - high.astype(jnp.float32)).astype(jnp.bfloat16)


def split3(a):
    high = a.astype(jnp.bfloat16)
    rest = a - high.astype(jnp.float32)
    return (high, *split(rest))


def mul(a, b):
    return jnp.dot(a, b, preferred_element_type=jnp.float32)


def split_kernel(a_ref, *outs):
    for out, value in zip(outs, split3(a_ref[...])):
        out[...] = value


def split_array(a):
    rows, cols = a.shape
    spec = pl.BlockSpec((rows // 4, cols), lambda i: (i, 0))
    return pl.pallas_call(
        split_kernel,
        grid=(4,),
        out_shape=(jax.ShapeDtypeStruct(a.shape, jnp.bfloat16),) * 3,
        in_specs=[spec],
        out_specs=(spec,) * 3,
        compiler_params=PARAMS,
        name="split",
    )(a)


def product(chunks, parts):
    left = jnp.concatenate([c[...] for c in chunks], axis=0)
    ph, pm, pl_ = parts
    step = 512
    total = None
    for k in range(0, left.shape[1], step):
        jh, jm, jl = split3(left[:, k:k + step])
        h, mid, low = ph[k:k + step, :], pm[k:k + step, :], pl_[k:k + step, :]
        term = mul(jh, h) + ((mul(jh, mid) + mul(jm, h)) + (mul(jh, low) + mul(jm, mid) + mul(jl, h)))
        total = term if total is None else total + term
    return total


def product_kernel(n, *refs):
    refs[n + 3][...] = product(refs[:n], refs[n:n + 3])


def multiply(chunks, parts):
    rows = sum(c.shape[0] for c in chunks)
    cols = parts[0].shape[1]
    work = 12 * rows * cols * parts[0].shape[0]
    return pl.pallas_call(
        functools.partial(product_kernel, len(chunks)),
        out_shape=jax.ShapeDtypeStruct((rows, cols), jnp.float32),
        in_specs=[VMEM] * (len(chunks) + 3),
        out_specs=VMEM,
        compiler_params=PARAMS,
        cost_estimate=pl.CostEstimate(flops=work, bytes_accessed=8 * 2**20, transcendentals=0),
        name="multiply",
    )(*chunks, *parts)


def runs(y, x, own):
    def start(half, dy, dx):
        spot = lax.rem(y + (dy + RING), RING) * RING + lax.rem(x + (dx + RING), RING)
        return (half * RING * RING + spot) * own

    first = lambda step: [start(0, SHIFT[step], d) for d in SHIFT]
    second = lambda step: [start(1, d, SHIFT[step]) for d in SHIFT]
    early = first(0) + second(0)
    middle = first(1) + first(2) + second(1) + second(2)
    late = first(3) + second(3)
    return early, middle, late


def last_kernel(at_ref, c0, c1, c2, c3, ph, pm, pl_, early_ref, middle_ref, out_ref, late_ref):
    late_ref[...] = product((c0, c1, c2, c3), (ph, pm, pl_))
    own = out_ref.shape[1] // (2 * RING * RING)
    z = at_ref[1]
    for ref, starts in zip((early_ref, middle_ref, late_ref), runs(at_ref[2], at_ref[3], own)):
        for i, start in enumerate(starts):
            rows = pl.ds(pl.multiple_of(start, own), own)
            for j in range(RING):
                lanes = pl.ds(pl.multiple_of(lax.rem(z + j, RING) * B, B), B)
                out_ref[j, rows, :] = ref[i * own:(i + 1) * own, lanes]


def multiply_last(at, chunks, parts, early, middle):
    rows = sum(c.shape[0] for c in chunks)
    cols = parts[0].shape[1]
    m = rows + early.shape[0] + middle.shape[0]
    return pl.pallas_call(
        last_kernel,
        out_shape=jax.ShapeDtypeStruct((RING, m, B), jnp.float32),
        in_specs=[SMEM] + [VMEM] * 9,
        out_specs=VMEM,
        scratch_shapes=[pltpu.VMEM((rows, cols), jnp.float32)],
        compiler_params=PARAMS,
        name="multiply_last",
    )(at, *chunks, *parts, early, middle)


def pick_kernel(at_ref, *refs):
    out_ref = refs[-1]
    own = out_ref.shape[0] // (2 * RING * RING)
    starts = sum(runs(at_ref[2], at_ref[3], own), [])
    i = 0
    for ref in refs[:-1]:
        for r in range(0, ref.shape[0], own):
            out_ref[pl.ds(pl.multiple_of(starts[i], own), own), :] = ref[r:r + own, :]
            i += 1


def pick(at, chunks):
    m = sum(c.shape[0] for c in chunks)
    block = lambda rows: pl.BlockSpec((rows, B), lambda i, at: (0, at[3] * RING + at[2]))
    return pl.pallas_call(
        pick_kernel,
        out_shape=jax.ShapeDtypeStruct((m, B), jnp.float32),
        grid_spec=pltpu.PrefetchScalarGridSpec(
            num_scalar_prefetch=1,
            grid=(1,),
            in_specs=[block(c.shape[0]) for c in chunks],
            out_specs=pl.BlockSpec((m, B), lambda i, at: (0, 0)),
        ),
        compiler_params=PARAMS,
        name="pick",
    )(at, *chunks)


def gram_kernel(at_ref, r0, r1, r2, r3, jac_ref, piece_ref, turned_ref, own_ref, other_ref):
    piece = (r0[...] + r1[...]) + (r2[...] + r3[...])
    piece_ref[...] = piece
    turned_ref[...] = piece.T
    half = own_ref.shape[0]
    for out, start in ((own_ref, at_ref[0] * half), (other_ref, (1 - at_ref[0]) * half)):
        out[...] = lax.dot_general(
            piece_ref[pl.ds(pl.multiple_of(start, half), half), :],
            jac_ref[...],
            (((1,), (1,)), ((), ())),
            precision=HI,
            preferred_element_type=jnp.float32,
        )


def gram(at, came, jac):
    m = jac.shape[0]
    shape = lambda *s: jax.ShapeDtypeStruct(s, jnp.float32)
    return pl.pallas_call(
        gram_kernel,
        out_shape=(shape(m, B), shape(B, m), shape(m // 2, m), shape(m // 2, m)),
        in_specs=[SMEM] + [VMEM] * 5,
        out_specs=(VMEM,) * 4,
        compiler_params=PARAMS,
        name="gram",
    )(at, *came, jac)


def final_kernel(
    at_ref, neg_ref, u_ref, p0, p1, p2, p3, rows_hbm, cov_hbm, new_hbm, delta_ref, cols, yh, yl, rows_ref, cov_ref, new_ref, sems
):
    count = cov_ref.shape[0]
    size = cov_ref.shape[1]
    block = lambda i: pl.ds(i * size, size)
    get_rows = [pltpu.make_async_copy(rows_hbm.at[:, i], rows_ref.at[i], sems.at[0, i]) for i in range(count)]
    get_cov = [pltpu.make_async_copy(cov_hbm.at[block(i)], cov_ref.at[i], sems.at[1, i]) for i in range(count)]
    put_new = [pltpu.make_async_copy(new_ref.at[i], new_hbm.at[block(i)], sems.at[2, i]) for i in range(count)]
    for i in range(count):
        get_rows[i].start()
        get_cov[i].start()
    for j, piece in enumerate((p0, p1, p2, p3)):
        place = lax.rem(at_ref[1] + (RING - j), RING)
        cols[:, pl.ds(pl.multiple_of(place * B, B), B)] = piece[...]
    yh[...], yl[...] = split(dot6(neg_ref[...], cols[...]))
    for i in range(count):
        get_rows[i].wait()
        rows = rows_ref[i].reshape(size, cols.shape[0])
        high, low = split(rows)
        change = mul(high, yh[...]) + (mul(high, yl[...]) + mul(low, yh[...]))
        get_cov[i].wait()
        new_ref[i] = (cov_ref[i] + change) * (1 / 0.98)
        put_new[i].start()
        scaled = rows * u_ref[...]
        lanes = sum(scaled[:, k:k + B] for k in range(0, rows.shape[1], B))
        for b in range(0, size, B):
            delta_ref[:, i * size + b:i * size + b + B] = jnp.sum(lanes[b:b + B, :].T, axis=0, keepdims=True)
    for i in range(count):
        put_new[i].wait()


def finish(at, neg, u, pieces, prod_rows, covariance):
    m = neg.shape[0]
    rows_dev, cols_dev = covariance.shape
    rows = rows_dev // RING
    hbm = pl.BlockSpec(memory_space=pltpu.HBM)
    new, delta = pl.pallas_call(
        final_kernel,
        out_shape=(
            jax.ShapeDtypeStruct((rows_dev, cols_dev), jnp.float32),
            jax.ShapeDtypeStruct((1, rows_dev), jnp.float32),
        ),
        in_specs=[SMEM] + [VMEM] * 6 + [hbm, hbm],
        out_specs=(hbm, VMEM),
        scratch_shapes=[
            pltpu.VMEM((m, cols_dev), jnp.float32),
            pltpu.VMEM((m, cols_dev), jnp.bfloat16),
            pltpu.VMEM((m, cols_dev), jnp.bfloat16),
            pltpu.VMEM((RING, RING, B, m), jnp.float32),
            pltpu.VMEM((RING, rows, cols_dev), jnp.float32),
            pltpu.VMEM((RING, rows, cols_dev), jnp.float32),
            pltpu.SemaphoreType.DMA((3, RING)),
        ],
        compiler_params=pltpu.CompilerParams(vmem_limit_bytes=52 * 2**20),
        name="finish",
    )(at, neg, u, *pieces, prod_rows.reshape(RING, RING, B, m), covariance)
    return delta.reshape(rows_dev), new


def halve_kernel(n0, n1, n2, n3, f0, f1, f2, f3):
    for near, far in ((n0, f0), (n1, f1), (n2, f2), (n3, f3)):
        far[...] = near[...]


def halves(near):
    rows, cols = near[0].shape
    block = lambda which: pl.BlockSpec((rows // 2, cols), lambda i: (which, 0))
    return pl.pallas_call(
        halve_kernel,
        grid=(1,),
        out_shape=(jax.ShapeDtypeStruct((rows // 2, cols), jnp.float32),) * 4,
        in_specs=[block(0), block(1), block(0), block(1)],
        out_specs=(block(0),) * 4,
        compiler_params=PARAMS,
        name="halves",
    )(*near)


def exchange(value, axes):
    return lax.all_to_all(value, axes, split_axis=0, concat_axis=0, tiled=True)


def shifted(value, axis, by):
    if axis == "row":
        return lax.ppermute(value, "row", [(i, (i + by) % RING) for i in range(RING)])
    spots = [(y, x) for y in range(RING) for x in range(RING)]
    if axis == "x":
        perm = [(y * RING + x, y * RING + (x + by) % RING) for y, x in spots]
    else:
        perm = [(y * RING + x, (y + by) % RING * RING + x) for y, x in spots]
    return lax.ppermute(value, "col", perm)


def tie(*values):
    return lax.optimization_barrier(values)


def both_ways(first, second, axes):
    near = tie(*[shifted(v, axis, by) for v, axis in zip((first, second), axes) for by in (1, -1)])
    part = halves(near)
    far = [shifted(part[i], axes[i // 2], (1, -1)[i % 2]) for i in range(4)]
    return near, far


def per_device(jacobian, covariance, noise, innovation):
    m = noise.shape[0]
    mine = jacobian.shape[0]
    rows_dev, cols_dev = covariance.shape
    g, z, col = lax.axis_index("grp"), lax.axis_index("row"), lax.axis_index("col")
    at = jnp.stack([g, z, col // RING, lax.rem(col, RING)]).astype(jnp.int32)
    reorder = lambda v: v.reshape(2, 4, 16, mine).transpose(0, 2, 1, 3).reshape(m)
    noise, innovation = reorder(noise), reorder(innovation)

    sent = jacobian.reshape(mine, 8, rows_dev).transpose(1, 0, 2)
    got = exchange(sent, ("grp", "row")).reshape(8 * mine, rows_dev)
    parts = split_array(covariance)
    half = 4 * mine
    a, b = got[:half], got[half:]
    near, far = both_ways(a, b, ("x", "y"))
    far = tie(*far)
    a4 = jnp.concatenate([a, near[0], near[1], far[0], far[1]], axis=0)
    b4 = jnp.concatenate([b, near[2], near[3], far[2], far[3]], axis=0)
    a4, b4 = tie(a4, b4)
    near, far = both_ways(a4, b4, ("y", "x"))
    early = multiply([a4, b4], parts)
    middle = multiply(near, parts)
    out = multiply_last(at, far, parts, early, middle)

    spots = [(a, b, x) for a in range(RING) for b in range(RING) for x in range(RING)]
    number = lambda a, b, x: (a * RING + b) * RING + x
    came = []
    for j in range(RING):
        perm = [(number(a, b, x), number(b, (a + j) % RING, x)) for a, b, x in spots]
        came.append(lax.ppermute(out[j], ("row", "col"), perm))
    jac = pick(at, [a4, b4, *near, *far])
    piece, turned, own, other = gram(at, came, jac)

    swap = [(0, 1), (1, 0)]
    h = m // 2
    own = own + lax.ppermute(other, "grp", swap)
    perm = [(number(a, b, x), number(b, a, x)) for a, b, x in spots]
    home = lax.ppermute(piece, ("row", "col"), perm)
    summed = exchange(own.reshape(64, h // 64, m), ("row", "col"))
    summed, turned = tie(summed, turned)
    prod_rows = lax.all_gather(turned, "col", axis=0)
    share = jnp.sum(summed, axis=0, keepdims=True)
    own = exchange(jnp.broadcast_to(share, (64, h // 64, m)), ("row", "col")).reshape(h, m)
    own, home = tie(own, home)
    other = lax.ppermute(own, "grp", swap)
    pieces = [home] + [shifted(home, "row", d) for d in (1, 2, 3)]
    neg, u = negative_inverse(at, own, other, noise.reshape(1, m), innovation.reshape(1, m))
    return finish(at, neg, u, pieces, prod_rows, covariance)


def solution(mesh):
    in_specs = (P(("grp", "row", "col"), None), P(("grp", "row"), "col"), P(), P())
    out_specs = (P(("grp", "row")), P(("grp", "row"), "col"))
    return jax.shard_map(
        per_device, mesh=mesh, in_specs=in_specs, out_specs=out_specs, check_vma=False
    )
```

```python
import functools

import jax
import jax.numpy as jnp
from jax import lax
from jax.experimental import pallas as pl
from jax.experimental.pallas import tpu as pltpu
from jax.sharding import PartitionSpec as P

HI = lax.Precision.HIGHEST
B = 128
Q = 8
RING = 4
SHIFT = (0, -1, 1, 2)


def dot6(a, b):
    return jnp.dot(a, b, precision=HI, preferred_element_type=jnp.float32)


def sweep_block(a):
    n = B // Q
    rows = [a[Q * i:Q * i + Q, :] for i in range(n)]
    lane = lax.broadcasted_iota(jnp.int32, (Q, B), 1)
    sub = lax.broadcasted_iota(jnp.int32, (Q, B), 0)
    for p in range(n):
        r = rows[p]
        cols = [jnp.broadcast_to(r[:, Q * p + j:Q * p + j + 1], (Q, B)) for j in range(Q)]
        for k in range(Q):
            pivot = jnp.broadcast_to(cols[k][k:k + 1, :], (Q, B))
            inv = pl.reciprocal(pivot, approx=True)
            inv = inv * (2.0 - pivot * inv)
            scaled = cols[k] * inv
            new = []
            for j in range(Q):
                if j == k:
                    new.append(jnp.where(sub == k, -inv, scaled))
                else:
                    row = jnp.broadcast_to(cols[j][k:k + 1, :], (Q, B))
                    new.append(jnp.where(sub == k, row * inv, cols[j] - scaled * row))
            row = jnp.broadcast_to(r[k:k + 1, :], (Q, B))
            r = jnp.where(sub == k, row * inv, r - scaled * row)
            cols = new
        for j in range(Q):
            r = jnp.where(lane == Q * p + j, cols[j], r)
        inside = (lane >= Q * p) & (lane < Q * p + Q)
        splat = [jnp.broadcast_to(r[j:j + 1, :], (Q, B)) for j in range(Q)]
        for b in [(p + 1 + i) % n for i in range(n - 1)]:
            old = rows[b]
            acc = jnp.where(inside, 0.0, old)
            for j in range(Q):
                acc = acc - jnp.broadcast_to(old[:, Q * p + j:Q * p + j + 1], (Q, B)) * splat[j]
            rows[b] = acc
        rows[p] = r
    return jnp.concatenate(rows, axis=0)


def sweep_all(out_ref, diag_ref, left_ref, turn_ref):
    m = out_ref.shape[0]
    n = m // B
    place = lambda k: pl.ds(pl.multiple_of(k * B, B), B)
    diag_ref[...] = out_ref[:B, :B]
    left_ref[...] = jnp.zeros_like(left_ref)
    turn_ref[...] = jnp.zeros_like(turn_ref)

    def update(k):
        last = place(jnp.maximum(k - 1, 0))
        lane = lax.broadcasted_iota(jnp.int32, (m, m), 1)
        inside = (lane >= (k - 1) * B) & (lane < k * B)
        out_ref[...] = jnp.where(inside, 0.0, out_ref[...]) - dot6(left_ref[...], turn_ref[...])
        out_ref[last, :] = jnp.where(k > 0, turn_ref[...], out_ref[last, :])

    def step(k, carry):
        neg = sweep_block(diag_ref[...])
        update(k)
        at, after = place(k), place(jnp.minimum(k + 1, n - 1))
        lane = lax.broadcasted_iota(jnp.int32, (B, m), 1)
        here = (lane >= k * B) & (lane < k * B + B)
        turn_ref[...] = jnp.where(here, jnp.concatenate([neg] * n, axis=1), -dot6(neg, out_ref[at, :]))
        left_ref[...] = out_ref[:, at]
        diag_ref[...] = out_ref[after, after] - dot6(left_ref[after, :], turn_ref[:, after])
        return carry

    lax.fori_loop(0, n, step, 0)
    update(n)


def inverse_kernel(at_ref, own_ref, other_ref, noise_ref, innov_ref, out_ref, u_ref, s_ref, *scratch):
    m = out_ref.shape[0]
    half = m // 2
    g = at_ref[0]
    s_ref[pl.ds(pl.multiple_of(g * half, half), half), :] = own_ref[...]
    s_ref[pl.ds(pl.multiple_of((1 - g) * half, half), half), :] = other_ref[...]
    diagonal = lax.broadcasted_iota(jnp.int32, (m, m), 0) == lax.broadcasted_iota(jnp.int32, (m, m), 1)
    s_ref[...] = s_ref[...] + jnp.where(diagonal, noise_ref[...], 0.0)
    out_ref[...] = s_ref[...]
    sweep_all(out_ref, *scratch)

    def apply(matrix_ref, row):
        column = jnp.broadcast_to(row, (B, m)).T
        parts = [jnp.sum(matrix_ref[:, i:i + B] * column, axis=0, keepdims=True) for i in range(0, m, B)]
        return jnp.concatenate(parts, axis=1)

    first = -apply(out_ref, innov_ref[...])
    rest = innov_ref[...] - apply(s_ref, first)
    u_ref[...] = first - apply(out_ref, rest)


VMEM = pl.BlockSpec(memory_space=pltpu.VMEM)
SMEM = pl.BlockSpec(memory_space=pltpu.SMEM)
PARAMS = pltpu.CompilerParams(vmem_limit_bytes=20 * 2**20)


def negative_inverse(at, own, other, noise, innovation):
    m = noise.shape[1]
    return pl.pallas_call(
        inverse_kernel,
        out_shape=(jax.ShapeDtypeStruct((m, m), jnp.float32), jax.ShapeDtypeStruct((1, m), jnp.float32)),
        in_specs=[SMEM] + [VMEM] * 4,
        out_specs=(VMEM, VMEM),
        scratch_shapes=[pltpu.VMEM(s, jnp.float32) for s in ((m, m), (B, B), (m, B), (B, m))],
        compiler_params=pltpu.CompilerParams(vmem_limit_bytes=16 * 2**20),
        cost_estimate=pl.CostEstimate(flops=25 * 10**9, bytes_accessed=2 * 2**20, transcendentals=0),
        name="inverse",
    )(at, own, other, noise, innovation)


def split(a):
    high = a.astype(jnp.bfloat16)
    return high, (a - high.astype(jnp.float32)).astype(jnp.bfloat16)


def split3(a):
    high = a.astype(jnp.bfloat16)
    rest = a - high.astype(jnp.float32)
    return (high, *split(rest))


def mul(a, b):
    return jnp.dot(a, b, preferred_element_type=jnp.float32)


def split_kernel(a_ref, *outs):
    for out, value in zip(outs, split3(a_ref[...])):
        out[...] = value


def split_array(a):
    rows, cols = a.shape
    spec = pl.BlockSpec((rows // 4, cols), lambda i: (i, 0))
    return pl.pallas_call(
        split_kernel,
        grid=(4,),
        out_shape=(jax.ShapeDtypeStruct(a.shape, jnp.bfloat16),) * 3,
        in_specs=[spec],
        out_specs=(spec,) * 3,
        compiler_params=PARAMS,
        name="split",
    )(a)


def product(chunks, parts):
    left = jnp.concatenate([c[...] for c in chunks], axis=0)
    ph, pm, pl_ = parts
    step = 512
    total = None
    for k in range(0, left.shape[1], step):
        jh, jm, jl = split3(left[:, k:k + step])
        h, mid, low = ph[k:k + step, :], pm[k:k + step, :], pl_[k:k + step, :]
        term = mul(jh, h) + ((mul(jh, mid) + mul(jm, h)) + (mul(jh, low) + mul(jm, mid) + mul(jl, h)))
        total = term if total is None else total + term
    return total


def product_kernel(n, *refs):
    refs[n + 3][...] = product(refs[:n], refs[n:n + 3])


def multiply(chunks, parts):
    rows = sum(c.shape[0] for c in chunks)
    cols = parts[0].shape[1]
    work = 12 * rows * cols * parts[0].shape[0]
    return pl.pallas_call(
        functools.partial(product_kernel, len(chunks)),
        out_shape=jax.ShapeDtypeStruct((rows, cols), jnp.float32),
        in_specs=[VMEM] * (len(chunks) + 3),
        out_specs=VMEM,
        compiler_params=PARAMS,
        cost_estimate=pl.CostEstimate(flops=work, bytes_accessed=8 * 2**20, transcendentals=0),
        name="multiply",
    )(*chunks, *parts)


def runs(y, x, own):
    def start(half, dy, dx):
        spot = lax.rem(y + (dy + RING), RING) * RING + lax.rem(x + (dx + RING), RING)
        return (half * RING * RING + spot) * own

    first = lambda step: [start(0, SHIFT[step], d) for d in SHIFT]
    second = lambda step: [start(1, d, SHIFT[step]) for d in SHIFT]
    early = first(0) + second(0)
    middle = first(1) + first(2) + second(1) + second(2)
    late = first(3) + second(3)
    return early, middle, late


def last_kernel(at_ref, c0, c1, c2, c3, ph, pm, pl_, early_ref, middle_ref, out_ref, late_ref):
    late_ref[...] = product((c0, c1, c2, c3), (ph, pm, pl_))
    own = out_ref.shape[1] // (2 * RING * RING)
    z = at_ref[1]
    for ref, starts in zip((early_ref, middle_ref, late_ref), runs(at_ref[2], at_ref[3], own)):
        for i, start in enumerate(starts):
            rows = pl.ds(pl.multiple_of(start, own), own)
            for j in range(RING):
                lanes = pl.ds(pl.multiple_of(lax.rem(z + j, RING) * B, B), B)
                out_ref[j, rows, :] = ref[i * own:(i + 1) * own, lanes]


def multiply_last(at, chunks, parts, early, middle):
    rows = sum(c.shape[0] for c in chunks)
    cols = parts[0].shape[1]
    m = rows + early.shape[0] + middle.shape[0]
    return pl.pallas_call(
        last_kernel,
        out_shape=jax.ShapeDtypeStruct((RING, m, B), jnp.float32),
        in_specs=[SMEM] + [VMEM] * 9,
        out_specs=VMEM,
        scratch_shapes=[pltpu.VMEM((rows, cols), jnp.float32)],
        compiler_params=PARAMS,
        name="multiply_last",
    )(at, *chunks, *parts, early, middle)


def pick_kernel(at_ref, *refs):
    out_ref = refs[-1]
    own = out_ref.shape[0] // (2 * RING * RING)
    starts = sum(runs(at_ref[2], at_ref[3], own), [])
    i = 0
    for ref in refs[:-1]:
        for r in range(0, ref.shape[0], own):
            out_ref[pl.ds(pl.multiple_of(starts[i], own), own), :] = ref[r:r + own, :]
            i += 1


def pick(at, chunks):
    m = sum(c.shape[0] for c in chunks)
    block = lambda rows: pl.BlockSpec((rows, B), lambda i, at: (0, at[3] * RING + at[2]))
    return pl.pallas_call(
        pick_kernel,
        out_shape=jax.ShapeDtypeStruct((m, B), jnp.float32),
        grid_spec=pltpu.PrefetchScalarGridSpec(
            num_scalar_prefetch=1,
            grid=(1,),
            in_specs=[block(c.shape[0]) for c in chunks],
            out_specs=pl.BlockSpec((m, B), lambda i, at: (0, 0)),
        ),
        compiler_params=PARAMS,
        name="pick",
    )(at, *chunks)


def gram_kernel(at_ref, r0, r1, r2, r3, jac_ref, piece_ref, turned_ref, own_ref, other_ref):
    piece = (r0[...] + r1[...]) + (r2[...] + r3[...])
    piece_ref[...] = piece
    turned_ref[...] = piece.T
    half = own_ref.shape[0]
    for out, start in ((own_ref, at_ref[0] * half), (other_ref, (1 - at_ref[0]) * half)):
        out[...] = lax.dot_general(
            piece_ref[pl.ds(pl.multiple_of(start, half), half), :],
            jac_ref[...],
            (((1,), (1,)), ((), ())),
            precision=HI,
            preferred_element_type=jnp.float32,
        )


def gram(at, came, jac):
    m = jac.shape[0]
    shape = lambda *s: jax.ShapeDtypeStruct(s, jnp.float32)
    return pl.pallas_call(
        gram_kernel,
        out_shape=(shape(m, B), shape(B, m), shape(m // 2, m), shape(m // 2, m)),
        in_specs=[SMEM] + [VMEM] * 5,
        out_specs=(VMEM,) * 4,
        compiler_params=PARAMS,
        name="gram",
    )(at, *came, jac)


def final_kernel(
    at_ref, neg_ref, u_ref, p0, p1, p2, p3, rows_hbm, cov_hbm, new_hbm, delta_ref, cols, yh, yl, rows_ref, cov_ref, new_ref, sems
):
    count = cov_ref.shape[0]
    size = cov_ref.shape[1]
    block = lambda i: pl.ds(i * size, size)
    get_rows = [pltpu.make_async_copy(rows_hbm.at[:, i], rows_ref.at[i], sems.at[0, i]) for i in range(count)]
    get_cov = [pltpu.make_async_copy(cov_hbm.at[block(i)], cov_ref.at[i], sems.at[1, i]) for i in range(count)]
    put_new = [pltpu.make_async_copy(new_ref.at[i], new_hbm.at[block(i)], sems.at[2, i]) for i in range(count)]
    for i in range(count):
        get_rows[i].start()
        get_cov[i].start()
    for j, piece in enumerate((p0, p1, p2, p3)):
        place = lax.rem(at_ref[1] + (RING - j), RING)
        cols[:, pl.ds(pl.multiple_of(place * B, B), B)] = piece[...]
    yh[...], yl[...] = split(dot6(neg_ref[...], cols[...]))
    for i in range(count):
        get_rows[i].wait()
        rows = rows_ref[i].reshape(size, cols.shape[0])
        high, low = split(rows)
        change = mul(high, yh[...]) + (mul(high, yl[...]) + mul(low, yh[...]))
        get_cov[i].wait()
        new_ref[i] = (cov_ref[i] + change) * (1 / 0.98)
        put_new[i].start()
        scaled = rows * u_ref[...]
        lanes = sum(scaled[:, k:k + B] for k in range(0, rows.shape[1], B))
        for b in range(0, size, B):
            delta_ref[:, i * size + b:i * size + b + B] = jnp.sum(lanes[b:b + B, :].T, axis=0, keepdims=True)
    for i in range(count):
        put_new[i].wait()


def finish(at, neg, u, pieces, prod_rows, covariance):
    m = neg.shape[0]
    rows_dev, cols_dev = covariance.shape
    rows = rows_dev // RING
    hbm = pl.BlockSpec(memory_space=pltpu.HBM)
    new, delta = pl.pallas_call(
        final_kernel,
        out_shape=(
            jax.ShapeDtypeStruct((rows_dev, cols_dev), jnp.float32),
            jax.ShapeDtypeStruct((1, rows_dev), jnp.float32),
        ),
        in_specs=[SMEM] + [VMEM] * 6 + [hbm, hbm],
        out_specs=(hbm, VMEM),
        scratch_shapes=[
            pltpu.VMEM((m, cols_dev), jnp.float32),
            pltpu.VMEM((m, cols_dev), jnp.bfloat16),
            pltpu.VMEM((m, cols_dev), jnp.bfloat16),
            pltpu.VMEM((RING, RING, B, m), jnp.float32),
            pltpu.VMEM((RING, rows, cols_dev), jnp.float32),
            pltpu.VMEM((RING, rows, cols_dev), jnp.float32),
            pltpu.SemaphoreType.DMA((3, RING)),
        ],
        compiler_params=pltpu.CompilerParams(vmem_limit_bytes=52 * 2**20),
        name="finish",
    )(at, neg, u, *pieces, prod_rows.reshape(RING, RING, B, m), covariance)
    return delta.reshape(rows_dev), new


def halve_kernel(n0, n1, n2, n3, f0, f1, f2, f3):
    for near, far in ((n0, f0), (n1, f1), (n2, f2), (n3, f3)):
        far[...] = near[...]


def halves(near):
    rows, cols = near[0].shape
    block = lambda which: pl.BlockSpec((rows // 2, cols), lambda i: (which, 0))
    return pl.pallas_call(
        halve_kernel,
        grid=(1,),
        out_shape=(jax.ShapeDtypeStruct((rows // 2, cols), jnp.float32),) * 4,
        in_specs=[block(0), block(1), block(0), block(1)],
        out_specs=(block(0),) * 4,
        compiler_params=PARAMS,
        name="halves",
    )(*near)


def exchange(value, axes):
    return lax.all_to_all(value, axes, split_axis=0, concat_axis=0, tiled=True)


def shifted(value, axis, by):
    if axis == "row":
        return lax.ppermute(value, "row", [(i, (i + by) % RING) for i in range(RING)])
    spots = [(y, x) for y in range(RING) for x in range(RING)]
    if axis == "x":
        perm = [(y * RING + x, y * RING + (x + by) % RING) for y, x in spots]
    else:
        perm = [(y * RING + x, (y + by) % RING * RING + x) for y, x in spots]
    return lax.ppermute(value, "col", perm)


def tie(*values):
    return lax.optimization_barrier(values)


def both_ways(first, second, axes):
    near = tie(*[shifted(v, axis, by) for v, axis in zip((first, second), axes) for by in (1, -1)])
    part = halves(near)
    far = [shifted(part[i], axes[i // 2], (1, -1)[i % 2]) for i in range(4)]
    return near, far


def per_device(jacobian, covariance, noise, innovation):
    m = noise.shape[0]
    mine = jacobian.shape[0]
    rows_dev, cols_dev = covariance.shape
    g, z, col = lax.axis_index("grp"), lax.axis_index("row"), lax.axis_index("col")
    at = jnp.stack([g, z, col // RING, lax.rem(col, RING)]).astype(jnp.int32)
    reorder = lambda v: v.reshape(2, 4, 16, mine).transpose(0, 2, 1, 3).reshape(m)
    noise, innovation = reorder(noise), reorder(innovation)

    sent = jacobian.reshape(mine, 8, rows_dev).transpose(1, 0, 2)
    got = exchange(sent, ("grp", "row")).reshape(8 * mine, rows_dev)
    parts = split_array(covariance)
    half = 4 * mine
    a, b = got[:half], got[half:]
    came = tie(*[shifted(v, axis, by) for v, axis in ((a, "x"), (b, "y")) for by in (1, -1, 2)])
    a4 = jnp.concatenate([a, *came[:3]], axis=0)
    b4 = jnp.concatenate([b, *came[3:]], axis=0)
    a4, b4 = tie(a4, b4)
    near, far = both_ways(a4, b4, ("y", "x"))
    early = multiply([a4, b4], parts)
    middle = multiply(near, parts)
    out = multiply_last(at, far, parts, early, middle)

    spots = [(a, b, x) for a in range(RING) for b in range(RING) for x in range(RING)]
    number = lambda a, b, x: (a * RING + b) * RING + x
    came = []
    for j in range(RING):
        perm = [(number(a, b, x), number(b, (a + j) % RING, x)) for a, b, x in spots]
        came.append(lax.ppermute(out[j], ("row", "col"), perm))
    jac = pick(at, [a4, b4, *near, *far])
    piece, turned, own, other = gram(at, came, jac)

    swap = [(0, 1), (1, 0)]
    h = m // 2
    own = own + lax.ppermute(other, "grp", swap)
    perm = [(number(a, b, x), number(b, a, x)) for a, b, x in spots]
    home = lax.ppermute(piece, ("row", "col"), perm)
    summed = exchange(own.reshape(64, h // 64, m), ("row", "col"))
    summed, turned = tie(summed, turned)
    prod_rows = lax.all_gather(turned, "col", axis=0)
    share = jnp.sum(summed, axis=0, keepdims=True)
    own = exchange(jnp.broadcast_to(share, (64, h // 64, m)), ("row", "col")).reshape(h, m)
    own, home = tie(own, home)
    other = lax.ppermute(own, "grp", swap)
    pieces = [home] + [shifted(home, "row", d) for d in (1, 2, 3)]
    neg, u = negative_inverse(at, own, other, noise.reshape(1, m), innovation.reshape(1, m))
    return finish(at, neg, u, pieces, prod_rows, covariance)


def solution(mesh):
    in_specs = (P(("grp", "row", "col"), None), P(("grp", "row"), "col"), P(), P())
    out_specs = (P(("grp", "row")), P(("grp", "row"), "col"))
    return jax.shard_map(
        per_device, mesh=mesh, in_specs=in_specs, out_specs=out_specs, check_vma=False
    )
```
